32 devices in a mesh: parts: 2 (over y), graph: 4 (over z), dp: 2 (over x), sub: 2 (over core).
Axes of the slice: x: 2, y: 2, z: 4, core: 2. Of those that a mesh axis runs over, the one named last changes fastest.
Arguments:
- node_feats: bfloat16 [4, 64, 3200], P(('parts', 'dp'), 'graph'), parts along dimension 0, may hold values from -6 to 6
- frame_blocks: bfloat16 [4, 1280, 165], P(('parts', 'dp'), ('graph', 'sub')), parts along dimension 0, may hold values from -4 to 4
- src_ids: int32 [4, 1280], P(('parts', 'dp'), ('graph', 'sub')), parts along dimension 0, may hold values from 0 to 63, as said below
- dst_ids: int32 [4, 1280], P(('parts', 'dp'), ('graph', 'sub')), parts along dimension 0, may hold values from 0 to 63, as said below
- edge_bias: float32 [4, 1280, 8], P(('parts', 'dp'), ('graph', 'sub')), parts along dimension 0, may hold values from -6 to 305
- w_zero: bfloat16 [640, 640], replicated, may hold values from -0.25 to 0.25
- w_one: bfloat16 [2, 512, 512], replicated, may hold values from -0.1875 to 0.1875
- w_two: bfloat16 [2, 384, 384], replicated, may hold values from -0.21875 to 0.21875
- alpha_w: bfloat16 [128, 8], replicated, may hold values from -0.5 to 0.5
- out_proj: bfloat16 [128, 128], replicated, may hold values from -1.5 to 1.5
- grad_out: bfloat16 [4, 64, 3200], P(('parts', 'dp'), 'graph'), parts along dimension 0, may hold values from -6 to 6
Outputs:
- updated: bfloat16 [4, 64, 3200], P(('parts', 'dp'), 'graph'), parts along dimension 0
- grad_nodes: float32 [4, 64, 3200], P(('parts', 'dp'), ('graph', 'sub')), parts along dimension 0
- grad_w_zero: float32 [1280, 640], P(('parts', 'graph', 'sub')), parts along dimension 0
- grad_w_one: float32 [4, 512, 512], P('parts', ('graph', 'sub')), parts along dimension 0
- grad_w_two: float32 [4, 384, 384], P('parts', ('graph', 'sub')), parts along dimension 0
- grad_alpha: float32 [256, 8], P(('parts', 'graph', 'sub')), parts along dimension 0
- grad_proj: float32 [256, 128], P(('parts', 'graph', 'sub')), parts along dimension 0
The draws below stay inside these ranges and needn't reach their ends.
There are 2 independent parts, one for each index of `parts`. The reference program is written for one: setup_inputs(seed, part) draws one part's arguments, and reference() takes and returns one part's arrays. A program takes and returns all parts, laid end to end along the dimension named above; an argument that names none is the same for every part. Nothing has to cross between parts.
Inputs may be any that keep to these rules, and one draw needn't show every extreme that they name: `dst_ids`: edges of a cell are ordered by destination; the edges at positions g * 20 * 16 to (g + 1) * 20 * 16 - 1 point at atoms g * 16 to (g + 1) * 16 - 1, and every atom has at least one edge. `src_ids`: an edge's source lies in the block of 16 atoms of its destination or in the block just before or after it, wrapping around the cell.
All inputs are finite; a program needn't handle non-finite values.
Results may differ from the reference program's by a relative error of at most 0.014.
Values may be sent and summed in bfloat16 or wider, within the bound.
A program may use at most 128 MiB of HBM per device.

```python
import jax
import jax.numpy as jnp
import numpy as np
from jax import lax

CHANNELS = 128
HEADS = 8
COEFS = 25
DEG = 20
NODE_DEV = 16
VALUES = 128
CELLS = 2
NODES = 64
EDGES = 1280
N_SUB = 2


def degree_scales():
    columns = []
    for degree in range(5):
        breadth = 2 * degree + 1
        columns = columns + [breadth ** (-0.5)] * (breadth * breadth)
    return np.array(columns, np.float32)


def draw_frame_blocks(key, part):
    key = jax.random.fold_in(key, 11)
    shape = (CELLS, EDGES, 165)
    base = jnp.clip(jax.random.normal(key, shape, jnp.float32), -4.0, 4.0)
    return (base * jnp.asarray(degree_scales())).astype(jnp.bfloat16)


def draw_dst_ids(key, part):
    key = jax.random.fold_in(key, 12)
    owners = NODES // NODE_DEV
    block_edges = DEG * NODE_DEV
    rising = jax.random.randint(key, (CELLS, owners, NODE_DEV), 0, DEG // 2)
    degrees = DEG + rising - jnp.roll(rising, 1, axis=2)
    bounds = jnp.cumsum(degrees, axis=2)
    position = jnp.arange(block_edges, dtype=jnp.int32)
    local_ids = jnp.sum((bounds[:, :, None, :] <= position[None, None, :, None]).astype(jnp.int32), axis=3)
    first_ids = jnp.arange(owners, dtype=jnp.int32)[None, :, None] * NODE_DEV
    return (local_ids + first_ids).reshape(CELLS, EDGES).astype(jnp.int32)


def draw_src_ids(key, part):
    key = jax.random.fold_in(key, 13)
    owners = NODES // NODE_DEV
    block_edges = DEG * NODE_DEV
    key_step, key_row = jax.random.split(key)
    stepping = jax.random.randint(key_step, (CELLS, owners, block_edges), -1, 2)
    row_ids = jax.random.randint(key_row, (CELLS, owners, block_edges), 0, NODE_DEV)
    owner_ids = jnp.arange(owners, dtype=jnp.int32)[None, :, None]
    sources = (owner_ids + stepping + owners) % owners * NODE_DEV + row_ids
    return sources.reshape(CELLS, EDGES).astype(jnp.int32)


def draw_edge_bias(key, part):
    key = jax.random.fold_in(key, 14)
    key_base = jax.random.fold_in(key, 0)
    shape = (CELLS, EDGES, HEADS)
    result = jnp.clip(jax.random.normal(key_base, shape, jnp.float32), -6.0, 6.0)
    return result.astype(jnp.float32)


def steps_of(rng, dims, cuts, smallest, top_value):
    level, own = 1.0, jax.random.fold_in(rng, 6)
    for dim, shards_of in cuts:
        draws = jnp.exp(jax.random.uniform(jax.random.fold_in(own, dim), (shards_of,), jnp.float32, smallest / len(cuts), top_value / len(cuts)))
        level = level * jnp.repeat(draws, dims[dim] // shards_of).reshape([-1 if axis == dim else 1 for axis in range(len(dims))])
    return level


def normal_values(rng, dims, scale, most, shards=(), held_as=jnp.bfloat16):
    values = jax.random.normal(rng, dims, jnp.float32) * scale
    if len(shards) > 0:
        values = steps_of(rng, dims, shards, -0.22, 0.18) * values
    return jnp.clip(values, min=-most, max=most).astype(held_as)


def setup_inputs(seed: int = 0, part: int = 0) -> dict:
    keys = jax.random.split(jax.random.key(seed), 12)
    own_keys = jax.random.split(jax.random.fold_in(keys[11], part), 12)
    return {
        "node_feats": normal_values(own_keys[0], (CELLS, NODES, COEFS * CHANNELS), 1.0, 6.0, ((0, 2), (1, 4))),
        "frame_blocks": draw_frame_blocks(jax.random.fold_in(jax.random.fold_in(keys[11], part), 71), part),
        "src_ids": draw_src_ids(jax.random.fold_in(jax.random.fold_in(keys[11], part), 71), part),
        "dst_ids": draw_dst_ids(jax.random.fold_in(jax.random.fold_in(keys[11], part), 71), part),
        "edge_bias": draw_edge_bias(jax.random.fold_in(jax.random.fold_in(keys[11], part), 71), part),
        "w_zero": normal_values(keys[5], (5 * CHANNELS, 5 * VALUES), (5 * CHANNELS) ** -0.5, 0.25),
        "w_one": normal_values(keys[6], (2, 4 * CHANNELS, 4 * VALUES), (8 * CHANNELS) ** -0.5, 0.1875),
        "w_two": normal_values(keys[7], (2, 3 * CHANNELS, 3 * VALUES), (6 * CHANNELS) ** -0.5, 0.21875),
        "alpha_w": normal_values(keys[8], (VALUES, HEADS), VALUES ** -0.5, 0.5),
        "out_proj": normal_values(keys[9], (VALUES, CHANNELS), (VALUES // 8) ** -0.5, 1.5),
        "grad_out": normal_values(own_keys[10], (CELLS, NODES, COEFS * CHANNELS), 1.0, 6.0, ((0, 2), (1, 4))),
    }


def contract(form, left, right):
    return jnp.einsum(form, left.astype(jnp.float32), right.astype(jnp.float32), precision=lax.Precision.HIGHEST)

def inner(left, right):
    return lax.dot_general(left, right, (((0,), (0,)), ((), ())), preferred_element_type=jnp.float32)

def across(left, right):
    return lax.dot_general(left, right, (((1,), (1,)), ((), ())), preferred_element_type=jnp.float32)

def frame_pieces(frames):
    pieces = []
    offset = 0
    for degree in range(5):
        breadth = 2 * degree + 1
        square = frames[:, offset:offset + breadth * breadth].reshape(-1, breadth, breadth)
        offset = offset + breadth * breadth
        reach = min(degree, 2)
        pieces.append(square[:, degree - reach:degree + reach + 1, :])
    return pieces

def degree_slice(matrix, degree, channels):
    return matrix[:, degree * degree * channels:(degree + 1) * (degree + 1) * channels].reshape(matrix.shape[0], 2 * degree + 1, channels)

def group_coeffs(pieces):
    centre = [min(degree, 2) for degree in range(5)]
    order_zero = jnp.concatenate([pieces[degree][:, centre[degree], :] for degree in range(5)], axis=1)
    order_one = jnp.concatenate([pieces[degree][:, centre[degree] + 1, :] for degree in range(1, 5)] + [pieces[degree][:, centre[degree] - 1, :] for degree in range(1, 5)], axis=1)
    order_two = jnp.concatenate([pieces[degree][:, 4, :] for degree in range(2, 5)] + [pieces[degree][:, 0, :] for degree in range(2, 5)], axis=1)
    return (order_zero, order_one, order_two)

def split_coeffs(order_zero, order_one, order_two, breadth):
    pieces = []
    for degree in range(5):
        stacked = [order_zero[:, degree * breadth:(degree + 1) * breadth]]
        if degree >= 1:
            stacked = [order_one[:, (3 + degree) * breadth:(4 + degree) * breadth]] + stacked + [order_one[:, (degree - 1) * breadth:degree * breadth]]
        if degree >= 2:
            stacked = [order_two[:, (1 + degree) * breadth:(2 + degree) * breadth]] + stacked + [order_two[:, (degree - 2) * breadth:(degree - 1) * breadth]]
        pieces.append(jnp.stack(stacked, axis=1))
    return pieces

def pair_matrix(weights):
    real_part = weights[0]
    imag_part = weights[1]
    return jnp.concatenate([jnp.concatenate([real_part, imag_part], axis=1), jnp.concatenate([-imag_part, real_part], axis=1)], axis=0)

def spread_heads(weights, value_ch):
    return jnp.repeat(weights, value_ch // weights.shape[1], axis=1)

def edge_forward(source_rows, pieces, w_zero, w_one, w_two, alpha_w, edge_bias):
    channels = source_rows.shape[1] // 25
    value_ch = w_zero.shape[1] // 5
    rotated = [contract('ekm,emc->ekc', pieces[degree], degree_slice(source_rows, degree, channels)).astype(jnp.bfloat16) for degree in range(5)]
    inputs = group_coeffs(rotated)
    out_zero = jnp.dot(inputs[0], w_zero, preferred_element_type=jnp.float32)
    out_one = jnp.dot(inputs[1], pair_matrix(w_one), preferred_element_type=jnp.float32)
    out_two = jnp.dot(inputs[2], pair_matrix(w_two), preferred_element_type=jnp.float32)
    scalar = out_zero[:, :value_ch]
    gate = jax.nn.silu(scalar).astype(jnp.bfloat16)
    logits = jnp.dot(gate, alpha_w, preferred_element_type=jnp.float32) + edge_bias
    values = split_coeffs(out_zero.astype(jnp.bfloat16), out_one.astype(jnp.bfloat16), out_two.astype(jnp.bfloat16), value_ch)
    return (inputs, scalar, gate, logits, values)

def rotate_back(weights, values, pieces):
    value_ch = values[0].shape[2]
    spread = spread_heads(weights, value_ch)[:, None, :]
    outputs = [contract('ekm,ekv->emv', pieces[degree], values[degree].astype(jnp.float32) * spread) for degree in range(5)]
    return jnp.concatenate([item.reshape(item.shape[0], -1) for item in outputs], axis=1)

def attention_grads(grad_back, values, pieces, heads):
    value_ch = values[0].shape[2]
    message_grads = [contract('ekm,emv->ekv', pieces[degree], degree_slice(grad_back, degree, value_ch)) for degree in range(5)]
    product = lax.optimization_barrier(jnp.sum(message_grads[0] * values[0].astype(jnp.float32), axis=1))
    for degree in range(1, 5):
        product = product + lax.optimization_barrier(jnp.sum(message_grads[degree] * values[degree].astype(jnp.float32), axis=1))
    head_grad = product.reshape(product.shape[0], heads, value_ch // heads).sum(axis=2)
    return (message_grads, head_grad)

def value_grads(message_grads, attention, logit_grad, scalar, alpha_w):
    value_ch = scalar.shape[1]
    spread = spread_heads(attention, value_ch)[:, None, :]
    grads = [item * spread for item in message_grads]
    order_zero, order_one, order_two = group_coeffs(grads)
    sigmoid = jax.nn.sigmoid(scalar)
    gate_grad = across(logit_grad, alpha_w) * sigmoid * (1.0 + scalar * (1.0 - sigmoid))
    order_zero = jnp.concatenate([order_zero[:, :value_ch] + gate_grad, order_zero[:, value_ch:]], axis=1)
    return (order_zero.astype(jnp.bfloat16), order_one.astype(jnp.bfloat16), order_two.astype(jnp.bfloat16))

def pair_grad(block, half_in, half_out):
    return jnp.stack([block[:half_in, :half_out] + block[half_in:, half_out:], block[:half_in, half_out:] - block[half_in:, :half_out]])

def row_gradients(grads, w_zero, w_one, w_two, pieces, channels):
    coeff_zero = across(grads[0], w_zero).astype(jnp.bfloat16)
    coeff_one = across(grads[1], pair_matrix(w_one)).astype(jnp.bfloat16)
    coeff_two = across(grads[2], pair_matrix(w_two)).astype(jnp.bfloat16)
    coeff_pieces = split_coeffs(coeff_zero, coeff_one, coeff_two, channels)
    return jnp.concatenate([contract('ekm,ekc->emc', pieces[degree], coeff_pieces[degree]).reshape(coeff_zero.shape[0], -1) for degree in range(5)], axis=1)

def weight_terms(inputs, grads, gate, logit_grad, summed_rows, grad_rows, w_one, w_two, value_ch, channels):
    weight_zero = inner(inputs[0], grads[0])
    weight_one = pair_grad(inner(inputs[1], grads[1]), w_one.shape[1], w_one.shape[2])
    weight_two = pair_grad(inner(inputs[2], grads[2]), w_two.shape[1], w_two.shape[2])
    alpha_grad = inner(gate, logit_grad)
    proj_grad = inner(summed_rows.reshape(-1, value_ch), grad_rows.reshape(-1, channels))
    return (weight_zero, weight_one, weight_two, alpha_grad, proj_grad)

def reference(node_feats, frame_blocks, src_ids, dst_ids, edge_bias, w_zero, w_one, w_two, alpha_w, out_proj, grad_out):
    channels = node_feats.shape[2] // 25
    value_ch = w_zero.shape[1] // 5
    heads = alpha_w.shape[1]
    owners = NODES // NODE_DEV
    block_edges = EDGES // owners
    halves = N_SUB
    half_edges = block_edges // halves
    half_nodes = NODE_DEV // halves

    def one_cell(cell_args):
        feats, frames, sources, targets, biases, upstream = cell_args

        def one_owner(carry, owner):
            row_total, weight_total = carry
            start = owner * block_edges
            frame_part = lax.dynamic_slice_in_dim(frames, start, block_edges, 0)
            source_part = lax.dynamic_slice_in_dim(sources, start, block_edges, 0)
            target_part = lax.dynamic_slice_in_dim(targets, start, block_edges, 0) - owner * NODE_DEV
            bias_part = lax.dynamic_slice_in_dim(biases, start, block_edges, 0)
            pieces = frame_pieces(frame_part)
            source_rows = jnp.take(feats, source_part, axis=0)
            inputs, scalar, gate, logits, values = edge_forward(source_rows, pieces, w_zero, w_one, w_two, alpha_w, bias_part)
            highest = jax.ops.segment_max(logits, target_part, num_segments=NODE_DEV, indices_are_sorted=True)
            raised = jnp.exp(logits - highest[target_part])
            totals = jax.ops.segment_sum(raised, target_part, num_segments=NODE_DEV, indices_are_sorted=True)
            attention = raised / totals[target_part]
            summed = jax.ops.segment_sum(rotate_back(attention, values, pieces), target_part, num_segments=NODE_DEV, indices_are_sorted=True)
            summed_half = summed.astype(jnp.bfloat16)
            own_rows = lax.dynamic_slice_in_dim(feats, owner * NODE_DEV, NODE_DEV, 0)
            projected = jnp.dot(summed_half.reshape(-1, value_ch), out_proj, preferred_element_type=jnp.float32).reshape(NODE_DEV, -1)
            updated = (own_rows.astype(jnp.float32) + projected).astype(jnp.bfloat16)
            own_grad = lax.dynamic_slice_in_dim(upstream, owner * NODE_DEV, NODE_DEV, 0)
            summed_grad = across(own_grad.reshape(-1, channels), out_proj).reshape(NODE_DEV, -1)
            message_grads, head_grad = attention_grads(summed_grad[target_part], values, pieces, heads)
            dots = jax.ops.segment_sum(attention * head_grad, target_part, num_segments=NODE_DEV, indices_are_sorted=True)
            logit_grad = (attention * (head_grad - dots[target_part])).astype(jnp.bfloat16)
            grads = value_grads(message_grads, attention, logit_grad, scalar, alpha_w)
            row_grads = row_gradients(grads, w_zero, w_one, w_two, pieces, channels)
            row_total = row_total.at[source_part].add(row_grads)
            for half in range(halves):
                edge_lo = half * half_edges
                edge_hi = edge_lo + half_edges
                node_lo = half * half_nodes
                node_hi = node_lo + half_nodes
                terms = weight_terms(tuple((item[edge_lo:edge_hi] for item in inputs)), tuple((item[edge_lo:edge_hi] for item in grads)), gate[edge_lo:edge_hi], logit_grad[edge_lo:edge_hi], summed_half[node_lo:node_hi], own_grad[node_lo:node_hi], w_one, w_two, value_ch, channels)
                rounded = tuple((lax.optimization_barrier(item.astype(jnp.bfloat16)).astype(jnp.float32) for item in terms))
                weight_total = tuple((before + after for before, after in zip(weight_total, rounded)))
            return ((row_total, weight_total), updated)
        start_weights = (jnp.zeros(w_zero.shape, jnp.float32), jnp.zeros(w_one.shape, jnp.float32), jnp.zeros(w_two.shape, jnp.float32), jnp.zeros(alpha_w.shape, jnp.float32), jnp.zeros(out_proj.shape, jnp.float32))
        start_rows = jnp.zeros((NODES, 25 * channels), jnp.float32)
        (row_total, weight_total), updated = lax.scan(one_owner, (start_rows, start_weights), jnp.arange(owners, dtype=jnp.int32))
        grad_rows = row_total + upstream.astype(jnp.float32)
        return (updated.reshape(NODES, -1), grad_rows) + weight_total
    results = lax.map(one_cell, (node_feats, frame_blocks, src_ids, dst_ids, edge_bias, grad_out))
    return (results[0], results[1], lax.optimization_barrier(jnp.sum(results[2], axis=0)), lax.optimization_barrier(jnp.sum(results[3], axis=0)), lax.optimization_barrier(jnp.sum(results[4], axis=0)), lax.optimization_barrier(jnp.sum(results[5], axis=0)), lax.optimization_barrier(jnp.sum(results[6], axis=0)))
```

```python
import jax
import jax.numpy as jnp
from jax import lax
from jax.experimental import pallas as pl
from jax.experimental.pallas import tpu as pltpu
from jax.sharding import PartitionSpec as P


def extended(block, sides, width):
    for axis, dim in sides:
        count = lax.axis_size(axis)
        forward = [(i, i + 1) for i in range(count - 1)]
        forward.append((count - 1, 0))
        backward = [(target, source) for source, target in forward]
        low = lax.ppermute(
            lax.slice_in_dim(block, block.shape[dim] - width, None, axis=dim), axis, forward
        )
        high = lax.ppermute(lax.slice_in_dim(block, 0, width, axis=dim), axis, backward)
        block = jnp.concatenate([low, block, high], axis=dim)
    return block


def combined_all(value, axis, join):
    pieces = jax.tree.map(lambda part: lax.all_gather(part, axis), value)
    head = jax.tree.map(lambda part: part[0], pieces)
    tail = jax.tree.map(lambda part: part[1:], pieces)
    running, _ = lax.scan(lambda running, section: (join(running, section), None), head, tail)
    return running


def passed_along(value, axis, by):
    peers = lax.axis_size(axis)
    return lax.ppermute(value, axis, [(i, (i + by) % peers) for i in range(peers)])


def contract(form, left, right):
    if left.dtype == right.dtype:
        return jnp.einsum(
            form, left, right, preferred_element_type=jnp.float32, precision=lax.Precision.HIGHEST
        )
    return jnp.einsum(form, left.astype(jnp.float32), right, precision=lax.Precision.HIGHEST)


def inner(left, right):
    return lax.dot_general(
        left, right, (((0,), (0,)), ((), ())), preferred_element_type=jnp.float32
    )


def across(left, right):
    return lax.dot_general(
        left, right, (((1,), (1,)), ((), ())), preferred_element_type=jnp.float32
    )


def frame_pieces(frames):
    pieces = []
    offset = 0
    for degree in range(5):
        breadth = 2 * degree + 1
        square = frames[:, offset : offset + breadth * breadth].reshape(-1, breadth, breadth)
        offset = offset + breadth * breadth
        reach = min(degree, 2)
        pieces.append(square[:, degree - reach : degree + reach + 1, :])
    return pieces


def degree_slice(matrix, degree, channels):
    return matrix[:, degree * degree * channels : (degree + 1) * (degree + 1) * channels].reshape(
        matrix.shape[0], 2 * degree + 1, channels
    )


def group_coeffs(pieces):
    centre = [min(degree, 2) for degree in range(5)]
    order_zero = jnp.concatenate(
        [pieces[degree][:, centre[degree], :] for degree in range(5)], axis=1
    )
    order_one = jnp.concatenate(
        [pieces[degree][:, centre[degree] + 1, :] for degree in range(1, 5)]
        + [pieces[degree][:, centre[degree] - 1, :] for degree in range(1, 5)],
        axis=1,
    )
    order_two = jnp.concatenate(
        [pieces[degree][:, 4, :] for degree in range(2, 5)]
        + [pieces[degree][:, 0, :] for degree in range(2, 5)],
        axis=1,
    )
    return (order_zero, order_one, order_two)


def split_coeffs(order_zero, order_one, order_two, breadth):
    pieces = []
    for degree in range(5):
        stacked = [order_zero[:, degree * breadth : (degree + 1) * breadth]]
        if degree >= 1:
            stacked = (
                [order_one[:, (3 + degree) * breadth : (4 + degree) * breadth]]
                + stacked
                + [order_one[:, (degree - 1) * breadth : degree * breadth]]
            )
        if degree >= 2:
            stacked = (
                [order_two[:, (1 + degree) * breadth : (2 + degree) * breadth]]
                + stacked
                + [order_two[:, (degree - 2) * breadth : (degree - 1) * breadth]]
            )
        pieces.append(jnp.stack(stacked, axis=1))
    return pieces


def pair_matrix(weights):
    real_part = weights[0]
    imag_part = weights[1]
    return jnp.concatenate(
        [
            jnp.concatenate([real_part, imag_part], axis=1),
            jnp.concatenate([-imag_part, real_part], axis=1),
        ],
        axis=0,
    )


def spread_heads(weights, value_ch):
    return jnp.repeat(weights, value_ch // weights.shape[1], axis=1)


def spread_rows(factor, value_ch):
    return jnp.tile(spread_heads(factor, value_ch), (1, 25))


def edge_forward(source_rows, pieces, w_zero, w_one, w_two, alpha_w, edge_bias):
    channels = source_rows.shape[1] // 25
    value_ch = w_zero.shape[1] // 5
    rotated = [
        contract(
            "ekm,emc->ekc", pieces[degree], degree_slice(source_rows, degree, channels)
        ).astype(jnp.bfloat16)
        for degree in range(5)
    ]
    inputs = group_coeffs(rotated)
    out_zero = jnp.dot(inputs[0], w_zero, preferred_element_type=jnp.float32)
    out_one = jnp.dot(inputs[1], pair_matrix(w_one), preferred_element_type=jnp.float32)
    out_two = jnp.dot(inputs[2], pair_matrix(w_two), preferred_element_type=jnp.float32)
    scalar = out_zero[:, :value_ch]
    gate = jax.nn.silu(scalar).astype(jnp.bfloat16)
    logits = jnp.dot(gate, alpha_w, preferred_element_type=jnp.float32) + edge_bias
    values = split_coeffs(
        out_zero.astype(jnp.bfloat16),
        out_one.astype(jnp.bfloat16),
        out_two.astype(jnp.bfloat16),
        value_ch,
    )
    return (inputs, scalar, gate, logits, values)


def rotate_back(weights, values, pieces):
    value_ch = values[0].shape[2]
    spread = spread_heads(weights, value_ch)[:, None, :]
    outputs = [
        contract("ekm,ekv->emv", pieces[degree], values[degree].astype(jnp.float32) * spread)
        for degree in range(5)
    ]
    return jnp.concatenate([item.reshape(item.shape[0], -1) for item in outputs], axis=1)


def attention_grads(grad_back, values, pieces, heads):
    value_ch = values[0].shape[2]
    message_grads = [
        contract("ekm,emv->ekv", pieces[degree], degree_slice(grad_back, degree, value_ch))
        for degree in range(5)
    ]
    product = jnp.sum(message_grads[0] * values[0].astype(jnp.float32), axis=1)
    for degree in range(1, 5):
        product = product + jnp.sum(
            message_grads[degree] * values[degree].astype(jnp.float32), axis=1
        )
    head_grad = product.reshape(product.shape[0], heads, value_ch // heads).sum(axis=2)
    return (message_grads, head_grad)


def value_grads(message_grads, attention, logit_grad, scalar, alpha_w):
    value_ch = scalar.shape[1]
    spread = spread_heads(attention, value_ch)[:, None, :]
    grads = [item * spread for item in message_grads]
    order_zero, order_one, order_two = group_coeffs(grads)
    sigmoid = jax.nn.sigmoid(scalar)
    gate_grad = across(logit_grad, alpha_w) * sigmoid * (1.0 + scalar * (1.0 - sigmoid))
    order_zero = jnp.concatenate(
        [order_zero[:, :value_ch] + gate_grad, order_zero[:, value_ch:]], axis=1
    )
    return (
        order_zero.astype(jnp.bfloat16),
        order_one.astype(jnp.bfloat16),
        order_two.astype(jnp.bfloat16),
    )


def pair_grad(block, half_in, half_out):
    return jnp.stack(
        [
            block[:half_in, :half_out] + block[half_in:, half_out:],
            block[:half_in, half_out:] - block[half_in:, :half_out],
        ]
    )


def input_grads(inputs, grads, w_zero, w_one, w_two, pieces, channels):
    weight_zero = inner(inputs[0], grads[0])
    weight_one = pair_grad(inner(inputs[1], grads[1]), w_one.shape[1], w_one.shape[2])
    weight_two = pair_grad(inner(inputs[2], grads[2]), w_two.shape[1], w_two.shape[2])
    coeff_zero = across(grads[0], w_zero).astype(jnp.bfloat16)
    coeff_one = across(grads[1], pair_matrix(w_one)).astype(jnp.bfloat16)
    coeff_two = across(grads[2], pair_matrix(w_two)).astype(jnp.bfloat16)
    coeff_pieces = split_coeffs(coeff_zero, coeff_one, coeff_two, channels)
    row_grads = jnp.concatenate(
        [
            contract("ekm,ekc->emc", pieces[degree], coeff_pieces[degree]).reshape(
                coeff_zero.shape[0], -1
            )
            for degree in range(5)
        ],
        axis=1,
    )
    return ((weight_zero, weight_one, weight_two), row_grads)


def grouped_rows(item, groups):
    if item.ndim == 3:
        return jnp.transpose(
            item.reshape(2, groups, item.shape[1] // groups, item.shape[2]), (1, 0, 2, 3)
        ).reshape(groups, -1)
    return item.reshape(groups, -1)


def body(
    node_feats,
    frame_blocks,
    src_ids,
    dst_ids,
    edge_bias,
    w_zero,
    w_one,
    w_two,
    alpha_w,
    out_proj,
    grad_out,
):
    tile_rows = node_feats.shape[1]
    channels = node_feats.shape[2] // 25
    value_ch = w_zero.shape[1] // 5
    heads = alpha_w.shape[1]
    owners = lax.axis_size("graph")
    owner = lax.axis_index("graph")
    padded = extended(node_feats, (("graph", 1),), tile_rows)[0]
    sources = src_ids[0]
    targets = dst_ids[0] - owner * tile_rows
    slots = (sources // tile_rows - owner + 1 + owners) % owners * tile_rows + sources % tile_rows
    pieces = frame_pieces(frame_blocks[0])
    source_rows = jnp.take(padded, slots, axis=0)
    inputs, scalar, gate, logits, values = edge_forward(
        source_rows, pieces, w_zero, w_one, w_two, alpha_w, edge_bias[0]
    )
    local_max = jnp.maximum(
        jax.ops.segment_max(logits, targets, num_segments=tile_rows, indices_are_sorted=True), -1e30
    )
    raised = jnp.exp(logits - local_max[targets])
    local_total = jax.ops.segment_sum(
        raised, targets, num_segments=tile_rows, indices_are_sorted=True
    )
    local_acc = jax.ops.segment_sum(
        rotate_back(raised, values, pieces),
        targets,
        num_segments=tile_rows,
        indices_are_sorted=True,
    )

    def combine(earlier, later):
        highest = jnp.maximum(earlier[0], later[0])
        left_scale = jnp.exp(earlier[0] - highest)
        right_scale = jnp.exp(later[0] - highest)
        return (
            highest,
            earlier[1] * left_scale + later[1] * right_scale,
            earlier[2] * spread_rows(left_scale, value_ch)
            + later[2] * spread_rows(right_scale, value_ch),
        )

    highest, totals, summed = combined_all((local_max, local_total, local_acc), "sub", combine)
    summed_half = (summed / spread_rows(totals, value_ch)).astype(jnp.bfloat16)
    attention = jnp.exp(logits - highest[targets]) / totals[targets]
    own_rows = node_feats[0]
    projected = jnp.dot(
        summed_half.reshape(-1, value_ch), out_proj, preferred_element_type=jnp.float32
    ).reshape(tile_rows, -1)
    updated = (own_rows.astype(jnp.float32) + projected).astype(jnp.bfloat16)
    own_grad = grad_out[0]
    half_rows = tile_rows // lax.axis_size("sub")
    half_start = lax.axis_index("sub") * half_rows
    summed_share = lax.dynamic_slice_in_dim(summed_half, half_start, half_rows, 0)
    grad_share = lax.dynamic_slice_in_dim(own_grad, half_start, half_rows, 0)
    proj_grad = inner(summed_share.reshape(-1, value_ch), grad_share.reshape(-1, channels))
    summed_grad = across(own_grad.reshape(-1, channels), out_proj).reshape(tile_rows, -1)
    message_grads, head_grad = attention_grads(summed_grad[targets], values, pieces, heads)
    local_dots = jax.ops.segment_sum(
        attention * head_grad, targets, num_segments=tile_rows, indices_are_sorted=True
    )
    dots = lax.psum(local_dots, "sub")
    logit_grad = (attention * (head_grad - dots[targets])).astype(jnp.bfloat16)
    alpha_grad = inner(gate, logit_grad)
    grads = value_grads(message_grads, attention, logit_grad, scalar, alpha_w)
    conv_grads, row_grads = input_grads(inputs, grads, w_zero, w_one, w_two, pieces, channels)
    buffer_grads = jax.ops.segment_sum(row_grads, slots, num_segments=3 * tile_rows)
    from_after = passed_along(buffer_grads[:tile_rows].astype(jnp.bfloat16), "graph", -1).astype(
        jnp.float32
    )
    from_before = passed_along(
        buffer_grads[2 * tile_rows :].astype(jnp.bfloat16), "graph", 1
    ).astype(jnp.float32)
    own_total = buffer_grads[tile_rows : 2 * tile_rows] + from_after + from_before
    node_share = lax.psum_scatter(
        own_total.astype(jnp.bfloat16), "sub", scatter_dimension=0, tiled=True
    ).astype(jnp.float32)
    grad_nodes = node_share + grad_share.astype(jnp.float32)
    terms = conv_grads + (alpha_grad, proj_grad)
    groups = lax.axis_size("graph") * lax.axis_size("sub")
    flattened = jnp.concatenate([grouped_rows(item, groups) for item in terms], axis=1)
    share = lax.psum_scatter(
        flattened.astype(jnp.bfloat16), ("graph", "sub"), scatter_dimension=0, tiled=True
    ).astype(jnp.float32)
    share = lax.psum(share.astype(jnp.bfloat16), "dp").astype(jnp.float32)[0]
    results = []
    offset = 0
    for item in terms:
        count = item.size // groups
        piece = share[offset : offset + count]
        if item.ndim == 3:
            results.append(piece.reshape(2, item.shape[1] // groups, item.shape[2]))
        else:
            results.append(piece.reshape(item.shape[0] // groups, item.shape[1]))
        offset = offset + count
    return (
        updated[None],
        grad_nodes[None],
        results[0],
        results[1],
        results[2],
        results[3],
        results[4],
    )


def column(degree, order):
    if order == 0:
        return degree
    if order == 1:
        return 5 + degree - 1
    if order == -1:
        return 9 + degree - 1
    if order == 2:
        return 13 + degree - 2
    return 16 + degree - 2


def frame_entries():
    entries = []
    offset = 0
    for degree in range(5):
        breadth = 2 * degree + 1
        reach = min(degree, 2)
        for order in range(-reach, reach + 1):
            for full in range(breadth):
                entries.append((degree, order, full, offset + (degree + order) * breadth + full))
        offset += breadth * breadth
    return entries


ENTRIES = frame_entries()
INDEX = {(d, o, f): i for i, (d, o, f, _) in enumerate(ENTRIES)}
LANES = 128
STEP = 16
F32 = jnp.float32
BF16 = jnp.bfloat16


def exact(left, right):
    return jnp.dot(left, right, preferred_element_type=F32, precision=lax.Precision.HIGHEST)


def fast(left, right):
    return jnp.dot(left, right, preferred_element_type=F32)


def lanes(index, count=1):
    return slice(index * LANES, (index + count) * LANES)


def fused(
    graphs, dps, parts,
    nf, fr, src, dst, bias, w0, w1, w2, aw, op, go,
    upd, gn, o0, o1, o2, oa, oproj,
    halo, small, small_in, acc_out, acc_in, fb, gp, sr, mg, zz, vv, weight, bk, gg, ig, rg, ng, ng_in,
    wg, r1, hh, r2, kk, r3, fin,
    halo_send, halo_recv, small_send, small_recv, acc_send, acc_recv, ng_send, ng_recv,
    s1s, s1r, s2s, s2r, s3s, s3r, s4s, s4r,
):
    edges = fr.shape[0]
    rows_dev = nf.shape[0]
    heads = aw.shape[1]
    g = lax.axis_index("graph")
    s = lax.axis_index("sub")
    d = lax.axis_index("dp")
    other = 1 - s

    def along(k):
        return lax.rem(g + k + graphs, graphs)

    def dp_along(k):
        return lax.rem(d + k, dps)

    def remote(source, target, send, recv, device):
        return pltpu.make_async_remote_copy(
            src_ref=source, dst_ref=target, send_sem=send, recv_sem=recv,
            device_id=device, device_id_type=pl.DeviceIdType.MESH,
        )

    barrier = pltpu.get_barrier_semaphore()
    peers = [{"sub": other}]
    for k in range(1, graphs):
        peers.append({"graph": along(k)})
    peers.append({"graph": along(1), "sub": other})
    peers.append({"graph": along(-1), "sub": other})
    for k in range(1, dps):
        peers.append({"dp": dp_along(k)})
    for peer in peers:
        pl.semaphore_signal(barrier, inc=1, device_id=peer, device_id_type=pl.DeviceIdType.MESH)
    pl.semaphore_wait(barrier, len(peers))

    halo_up = remote(nf, halo.at[0], halo_send.at[0], halo_recv.at[0], {"graph": along(1)})
    halo_down = remote(nf, halo.at[1], halo_send.at[1], halo_recv.at[1], {"graph": along(-1)})
    halo_up.start()
    halo_down.start()

    src_row = src[...]
    dst_row = dst[...]
    eye = lax.broadcasted_iota(jnp.int32, (edges, edges), 0) == lax.broadcasted_iota(
        jnp.int32, (edges, edges), 1
    )

    def to_column(row):
        spread = jnp.where(eye, jnp.broadcast_to(row.astype(F32), (edges, edges)), 0.0)
        return jnp.sum(spread, axis=1, keepdims=True).astype(jnp.int32)

    src_col = to_column(src_row)
    dst_col = to_column(dst_row) - g * rows_dev
    lane48 = lax.broadcasted_iota(jnp.int32, (edges, 3 * rows_dev), 1)
    row48 = lax.broadcasted_iota(jnp.int32, (3 * rows_dev, edges), 0)

    def block_ids(position):
        low = along(-1) * rows_dev + position
        mid = g * rows_dev + position - rows_dev
        high = along(1) * rows_dev + position - 2 * rows_dev
        return jnp.where(
            position < rows_dev, low, jnp.where(position < 2 * rows_dev, mid, high)
        )

    def hot(match, dtype=BF16):
        return jnp.where(match, 1.0, 0.0).astype(dtype)

    pick_src = hot(block_ids(lane48) == src_col)
    put_src = hot(block_ids(row48) == src_row)
    pick_dst = hot(lax.broadcasted_iota(jnp.int32, (edges, rows_dev), 1) == dst_col)
    put_dst = hot(
        lax.broadcasted_iota(jnp.int32, (rows_dev, edges), 0) == dst_row - g * rows_dev
    )
    lane_j = lax.broadcasted_iota(jnp.int32, (edges, LANES), 1)
    mine = lax.shift_right_logical(lane_j, 3) == dst_col
    sq0 = lax.broadcasted_iota(jnp.int32, (LANES, LANES), 0)
    sq1 = lax.broadcasted_iota(jnp.int32, (LANES, LANES), 1)
    spread = hot(jnp.bitwise_and(sq0, 7) == lax.shift_right_logical(sq1, 4), F32)
    gather_heads = hot(lax.shift_right_logical(sq0, 4) == jnp.bitwise_and(sq1, 7), F32)
    compact = hot(jnp.bitwise_and(sq0, 7) == sq1)
    tile_heads = hot(
        lax.broadcasted_iota(jnp.int32, (heads, LANES), 0)
        == jnp.bitwise_and(lax.broadcasted_iota(jnp.int32, (heads, LANES), 1), 7),
        F32,
    )
    alpha_t = fast(aw[...], tile_heads.astype(BF16)).astype(BF16)
    proj = op[...]

    for k in range(25):
        rows = fast(pick_dst, go[:, lanes(k)]).astype(BF16)
        gp[:, lanes(k)] = across(rows, proj)

    def message_step(c, _):
        at = pl.ds(pl.multiple_of(c * STEP, STEP), STEP)
        frames = fr[at, :].astype(F32)
        for degree in range(5):
            reach = min(degree, 2)
            breadth = 2 * degree + 1
            inputs = [gp[at, lanes(degree * degree + f)] for f in range(breadth)]
            for order in range(-reach, reach + 1):
                total = None
                for f in range(breadth):
                    i = INDEX[(degree, order, f)]
                    col = ENTRIES[i][3]
                    value = jnp.broadcast_to(frames[:, col : col + 1], (STEP, LANES))
                    fb[i, at, :] = value
                    term = value * inputs[f]
                    total = term if total is None else total + term
                mg[at, lanes(column(degree, order))] = total
        return 0

    lax.fori_loop(0, edges // STEP, message_step, 0)

    halo_up.wait()
    halo_down.wait()
    for k in range(25):
        block = jnp.concatenate([halo[0, :, lanes(k)], nf[:, lanes(k)], halo[1, :, lanes(k)]], axis=0)
        sr[:, lanes(k)] = fast(pick_src, block)

    def rotate_step(c, _):
        at = pl.ds(pl.multiple_of(c * STEP, STEP), STEP)
        for degree in range(5):
            reach = min(degree, 2)
            breadth = 2 * degree + 1
            inputs = [sr[at, lanes(degree * degree + f)] for f in range(breadth)]
            for order in range(-reach, reach + 1):
                total = None
                for f in range(breadth):
                    term = fb[INDEX[(degree, order, f)], at, :] * inputs[f]
                    total = term if total is None else total + term
                zz[at, lanes(column(degree, order))] = total.astype(BF16)
        return 0

    lax.fori_loop(0, edges // STEP, rotate_step, 0)

    z0 = zz[:, lanes(0, 5)]
    zp1, zm1 = zz[:, lanes(5, 4)], zz[:, lanes(9, 4)]
    zp2, zm2 = zz[:, lanes(13, 3)], zz[:, lanes(16, 3)]
    y0 = fast(z0, w0[...])
    scalar = y0[:, :LANES]
    vv[:, lanes(0, 5)] = y0.astype(BF16)
    vv[:, lanes(5, 4)] = (fast(zp1, w1[0]) - fast(zm1, w1[1])).astype(BF16)
    vv[:, lanes(9, 4)] = (fast(zp1, w1[1]) + fast(zm1, w1[0])).astype(BF16)
    vv[:, lanes(13, 3)] = (fast(zp2, w2[0]) - fast(zm2, w2[1])).astype(BF16)
    vv[:, lanes(16, 3)] = (fast(zp2, w2[1]) + fast(zm2, w2[0])).astype(BF16)
    sigmoid = lax.logistic(scalar)
    gate = (scalar * sigmoid).astype(BF16)
    logits = fast(gate, alpha_t) + exact(bias[...], tile_heads)
    logits = jnp.where(mine, logits, -1e30)
    product = None
    for k in range(19):
        term = mg[:, lanes(k)] * vv[:, lanes(k)].astype(F32)
        product = term if product is None else product + term
    head_grad = exact(product, gather_heads)
    peak = jnp.max(logits, axis=0, keepdims=True)
    raised = jnp.where(mine, jnp.exp(logits - peak), 0.0)
    total = jnp.sum(raised, axis=0, keepdims=True)
    dots = jnp.sum(raised * head_grad, axis=0, keepdims=True)
    small[0:1, :] = peak
    small[1:2, :] = total
    small[2:3, :] = dots
    small[3:8, :] = jnp.zeros((5, LANES), F32)
    small_copy = remote(small, small_in, small_send, small_recv, {"sub": other})
    small_copy.start()

    weight[...] = exact(raised, spread)

    def back_step(c, _):
        at = pl.ds(pl.multiple_of(c * STEP, STEP), STEP)
        scale = weight[at, :]
        for degree in range(5):
            reach = min(degree, 2)
            orders = range(-reach, reach + 1)
            inputs = {o: vv[at, lanes(column(degree, o))].astype(F32) * scale for o in orders}
            for f in range(2 * degree + 1):
                out = None
                for o in orders:
                    term = fb[INDEX[(degree, o, f)], at, :] * inputs[o]
                    out = term if out is None else out + term
                bk[at, lanes(degree * degree + f)] = out.astype(BF16)
        return 0

    lax.fori_loop(0, edges // STEP, back_step, 0)
    small_copy.wait()
    peak_in = small_in[0:1, :]
    top = jnp.maximum(peak, peak_in)
    own_scale = jnp.exp(peak - top)
    in_scale = jnp.exp(peak_in - top)
    whole = total * own_scale + small_in[1:2, :] * in_scale
    all_dots = (dots * own_scale + small_in[2:3, :] * in_scale) / whole
    node_lane = lax.broadcasted_iota(jnp.int32, (rows_dev, LANES), 1)
    node_row = lax.broadcasted_iota(jnp.int32, (rows_dev, LANES), 0)
    node_scale = exact(
        jnp.where(lax.shift_right_logical(node_lane, 3) == node_row, own_scale / whole, 0.0), spread
    )
    for k in range(25):
        acc_out[:, lanes(k)] = fast(put_dst, bk[:, lanes(k)]) * node_scale
    acc_copy = remote(acc_out, acc_in, acc_send, acc_recv, {"sub": other})
    acc_copy.start()

    attention = raised * (own_scale / whole)
    logit_grad = (attention * (head_grad - all_dots)).astype(BF16)
    spread_att = exact(attention, spread)
    gate_grad = across(logit_grad, alpha_t) * sigmoid * (1.0 + scalar * (1.0 - sigmoid))
    for k in range(19):
        grad = mg[:, lanes(k)] * spread_att
        if k == 0:
            grad = grad + gate_grad
        gg[:, lanes(k)] = grad.astype(BF16)

    groups = graphs * 2

    def put(piece, base, rows_share, row0, matrix):
        wide = matrix.shape[1] // LANES
        part = wg[piece].shape[3]
        for i in range(matrix.shape[0] // STEP):
            row = row0 + i * STEP
            group = row // rows_share
            inner_row = (row % rows_share) // STEP
            for j in range(wide):
                tile = base + inner_row * wide + j
                wg[piece][group % 2, tile // part, group // 2, tile % part] = matrix[
                    i * STEP : (i + 1) * STEP, lanes(j)
                ].astype(BF16)

    def zero_tail(piece, used):
        part = wg[piece].shape[3]
        for tile in range(used, part * dps):
            wg[piece][:, tile // part, :, tile % part] = jnp.zeros((2, graphs, STEP, LANES), BF16)

    def stage_one(piece):
        return remote(
            wg[piece].at[other], r1[piece], s1s.at[piece], s1r.at[piece], {"sub": other}
        )

    def stage_two(piece):
        return [
            remote(
                hh[piece].at[dp_along(k)], r2[piece].at[k - 1],
                s2s.at[piece, k - 1], s2r.at[piece, k - 1], {"dp": dp_along(k)},
            )
            for k in range(1, dps)
        ]

    def stage_three(piece):
        return [
            remote(
                kk[piece].at[along(k)], r3[piece].at[k - 1],
                s3s.at[piece, k - 1], s3r.at[piece, k - 1], {"graph": along(k)},
            )
            for k in range(1, graphs)
        ]

    def stage_four(piece):
        return [
            remote(
                fin[piece].at[0], fin[piece].at[k],
                s4s.at[piece, k - 1], s4r.at[piece, k - 1], {"dp": dp_along(k)},
            )
            for k in range(1, dps)
        ]

    def start(copies):
        for copy in copies:
            copy.start()
        return copies

    def wait(copies):
        for copy in copies:
            copy.wait()

    gp1, gm1 = gg[:, lanes(5, 4)], gg[:, lanes(9, 4)]
    rows1 = 512 // groups
    for b in range(4):
        zp, zm = zz[:, lanes(5 + b)], zz[:, lanes(9 + b)]
        base = (rows1 // STEP) * 4
        put(0, 0, rows1, b * LANES, inner(zp, gp1) + inner(zm, gm1))
        put(0, base, rows1, b * LANES, inner(zp, gm1) - inner(zm, gp1))
    zero_tail(0, 2 * (rows1 // STEP) * 4)
    one = [None] * 3
    one[0] = stage_one(0)
    one[0].start()

    g0 = gg[:, lanes(0, 5)]
    rows0 = 640 // groups
    for b in range(5):
        put(1, 0, rows0, b * LANES, inner(zz[:, lanes(b)], g0))
    alpha_rows = LANES // groups
    tiles0 = (rows0 // STEP) * 5
    logit_small = fast(logit_grad, compact).astype(BF16)
    put(1, tiles0, alpha_rows, 0, inner(gate, logit_small))
    zero_tail(1, tiles0 + alpha_rows // STEP)
    one[1] = stage_one(1)
    one[1].start()

    acc_copy.wait()
    summed = jnp.concatenate(
        [(acc_out[:, lanes(k)] + acc_in[:, lanes(k)]).astype(BF16) for k in range(25)], axis=0
    )
    projected = fast(summed, proj)
    for k in range(25):
        upd[:, lanes(k)] = (
            nf[:, lanes(k)].astype(F32) + projected[k * rows_dev : (k + 1) * rows_dev]
        ).astype(BF16)
    cotangent = jnp.concatenate([go[:, lanes(k)] for k in range(25)], axis=0)
    half = rows_dev // 2
    in_half = lax.broadcasted_iota(jnp.int32, summed.shape, 0)
    in_half = lax.shift_right_logical(jnp.bitwise_and(in_half, rows_dev - 1), 3) == s
    share = jnp.where(in_half, summed.astype(F32), 0.0).astype(BF16)
    gp2, gm2 = gg[:, lanes(13, 3)], gg[:, lanes(16, 3)]
    rows2 = 384 // groups
    tiles2 = (rows2 // STEP) * 3
    for b in range(3):
        zp, zm = zz[:, lanes(13 + b)], zz[:, lanes(16 + b)]
        put(2, 0, rows2, b * LANES, inner(zp, gp2) + inner(zm, gm2))
        put(2, tiles2, rows2, b * LANES, inner(zp, gm2) - inner(zm, gp2))
    put(2, 2 * tiles2, alpha_rows, 0, inner(share, cotangent))
    zero_tail(2, 2 * tiles2 + alpha_rows // STEP)
    one[2] = stage_one(2)
    one[2].start()

    def add_one(piece):
        one[piece].wait()
        for p in range(dps):
            hh[piece][p] = (wg[piece][s, p].astype(F32) + r1[piece][p].astype(F32)).astype(BF16)
        return start(stage_two(piece))

    def add_two(piece):
        wait(two[piece])
        value = hh[piece][d].astype(F32)
        for k in range(1, dps):
            value = value + r2[piece][k - 1].astype(F32)
        kk[piece][...] = value.astype(BF16)
        return start(stage_three(piece))

    def add_three(piece):
        wait(three[piece])
        value = kk[piece][g].astype(F32)
        for k in range(1, graphs):
            value = value + r3[piece][k - 1].astype(F32)
        fin[piece][0] = value.astype(BF16)
        return start(stage_four(piece))

    two = [None] * 3
    three = [None] * 3
    four = [None] * 3
    two[0] = add_one(0)
    two[1] = add_one(1)

    ig[:, lanes(0, 5)] = across(g0, w0[...]).astype(BF16)
    ig[:, lanes(5, 4)] = (across(gp1, w1[0]) + across(gm1, w1[1])).astype(BF16)
    ig[:, lanes(9, 4)] = (across(gm1, w1[0]) - across(gp1, w1[1])).astype(BF16)
    two[2] = add_one(2)
    ig[:, lanes(13, 3)] = (across(gp2, w2[0]) + across(gm2, w2[1])).astype(BF16)
    ig[:, lanes(16, 3)] = (across(gm2, w2[0]) - across(gp2, w2[1])).astype(BF16)

    def row_step(c, _):
        at = pl.ds(pl.multiple_of(c * STEP, STEP), STEP)
        for degree in range(5):
            reach = min(degree, 2)
            orders = range(-reach, reach + 1)
            inputs = {o: ig[at, lanes(column(degree, o))].astype(F32) for o in orders}
            for f in range(2 * degree + 1):
                out = None
                for o in orders:
                    term = fb[INDEX[(degree, o, f)], at, :] * inputs[o]
                    out = term if out is None else out + term
                rg[at, lanes(degree * degree + f)] = out.astype(BF16)
        return 0

    lax.fori_loop(0, edges // STEP, row_step, 0)

    for k in range(13):
        low = fast(put_src, rg[:, lanes(k)])
        high = fast(put_src, rg[:, lanes(13 + k)]) if k < 12 else jnp.zeros_like(low)
        for b in range(3):
            for h in range(2):
                at = slice(b * rows_dev + h * half, b * rows_dev + (h + 1) * half)
                ng[b, h, :, lanes(k)] = jnp.concatenate([low[at], high[at]], axis=0).astype(BF16)
    node_copies = []
    for b in range(3):
        for r in range(2):
            if b == 1 and r == 0:
                continue
            to = lax.rem(s + r, 2)
            node_copies.append(
                remote(
                    ng.at[b, to], ng_in.at[b, r], ng_send.at[b, r], ng_recv.at[b, r],
                    {"graph": along(b - 1), "sub": to},
                )
            )
    start(node_copies)

    three[0] = add_two(0)
    three[1] = add_two(1)
    three[2] = add_two(2)

    wait(node_copies)
    for k in range(13):
        value = ng[1, s, :, lanes(k)].astype(F32)
        for b in range(3):
            for r in range(2):
                if b == 1 and r == 0:
                    continue
                value = value + ng_in[b, r, :, lanes(k)].astype(F32)
        for part, coef in ((0, k), (1, 13 + k)):
            if coef < 25:
                base = go[:, lanes(coef)].astype(F32)
                base = jnp.where(s == 0, base[:half], base[half:])
                gn[:, lanes(coef)] = value[part * half : (part + 1) * half] + base

    def take(piece, tile):
        part = fin[piece].shape[1]
        slot = lax.rem(d - tile // part + dps, dps)
        return fin[piece][slot, tile % part].astype(F32)

    four[0] = add_three(0)
    four[1] = add_three(1)
    wait(four[0])
    for q in range(2):
        for i in range(rows1 // STEP):
            for j in range(4):
                tile = q * (rows1 // STEP) * 4 + i * 4 + j
                o1[q, i * STEP : (i + 1) * STEP, lanes(j)] = take(0, tile)
    wait(four[1])
    for i in range(rows0 // STEP):
        for j in range(5):
            o0[i * STEP : (i + 1) * STEP, lanes(j)] = take(1, i * 5 + j)
    for i in range(alpha_rows // STEP):
        oa[i * STEP : (i + 1) * STEP, :] = take(1, tiles0 + i)[:, :heads]
    four[2] = add_three(2)
    wait(four[2])
    for q in range(2):
        for i in range(rows2 // STEP):
            for j in range(3):
                o2[q, i * STEP : (i + 1) * STEP, lanes(j)] = take(2, q * tiles2 + i * 3 + j)
    for i in range(alpha_rows // STEP):
        oproj[i * STEP : (i + 1) * STEP, :] = take(2, 2 * tiles2 + i)


def fused_body(graphs, dps, parts):
    groups = graphs * 2

    def run(node_feats, frame_blocks, src_ids, dst_ids, edge_bias, w_zero, w_one, w_two, alpha_w, out_proj, grad_out):
        rows_dev = node_feats.shape[1]
        edges = frame_blocks.shape[1]
        heads = alpha_w.shape[1]
        used = (
            2 * (512 // groups // STEP) * 4,
            (640 // groups // STEP) * 5 + LANES // groups // STEP,
            2 * (384 // groups // STEP) * 3 + LANES // groups // STEP,
        )
        part = [-(-count // dps) for count in used]
        dma = pltpu.SemaphoreType.DMA
        wide = 25 * LANES
        kept = 19 * LANES

        def per_piece(lead):
            return [pltpu.VMEM((*lead(p), STEP, LANES), BF16) for p in part]

        scratch = [
            pltpu.VMEM((2, rows_dev, wide), BF16),
            pltpu.VMEM((8, LANES), F32),
            pltpu.VMEM((8, LANES), F32),
            pltpu.VMEM((rows_dev, wide), F32),
            pltpu.VMEM((rows_dev, wide), F32),
            pltpu.VMEM((len(ENTRIES), edges, LANES), F32),
            pltpu.VMEM((edges, wide), F32),
            pltpu.VMEM((edges, wide), F32),
            pltpu.VMEM((edges, kept), F32),
            pltpu.VMEM((edges, kept), BF16),
            pltpu.VMEM((edges, kept), BF16),
            pltpu.VMEM((edges, LANES), F32),
            pltpu.VMEM((edges, wide), BF16),
            pltpu.VMEM((edges, kept), BF16),
            pltpu.VMEM((edges, kept), BF16),
            pltpu.VMEM((edges, wide), BF16),
            pltpu.VMEM((3, 2, STEP, 13 * LANES), BF16),
            pltpu.VMEM((3, 2, STEP, 13 * LANES), BF16),
            per_piece(lambda p: (2, dps, graphs, p)),
            per_piece(lambda p: (dps, graphs, p)),
            per_piece(lambda p: (dps, graphs, p)),
            per_piece(lambda p: (max(dps - 1, 1), graphs, p)),
            per_piece(lambda p: (graphs, p)),
            per_piece(lambda p: (graphs - 1, p)),
            per_piece(lambda p: (dps, p)),
            dma((2,)), dma((2,)), dma, dma, dma, dma, dma((3, 2)), dma((3, 2)),
            dma((3,)), dma((3,)),
            dma((3, max(dps - 1, 1))), dma((3, max(dps - 1, 1))),
            dma((3, graphs - 1)), dma((3, graphs - 1)),
            dma((3, max(dps - 1, 1))), dma((3, max(dps - 1, 1))),
        ]
        flat = []
        counts = []
        for item in scratch:
            if isinstance(item, list):
                counts.append(len(item))
                flat.extend(item)
            else:
                counts.append(0)
                flat.append(item)

        def entry(*refs):
            lead, rest = refs[:18], list(refs[18:])
            grouped = []
            for count in counts:
                if count:
                    grouped.append(rest[:count])
                    rest = rest[count:]
                else:
                    grouped.append(rest.pop(0))
            fused(graphs, dps, parts, *lead, *grouped)

        vmem = pl.BlockSpec(memory_space=pltpu.VMEM)
        out = pl.pallas_call(
            entry,
            out_shape=(
                jax.ShapeDtypeStruct((rows_dev, wide), BF16),
                jax.ShapeDtypeStruct((rows_dev // 2, wide), F32),
                jax.ShapeDtypeStruct((640 // groups, 640), F32),
                jax.ShapeDtypeStruct((2, 512 // groups, 512), F32),
                jax.ShapeDtypeStruct((2, 384 // groups, 384), F32),
                jax.ShapeDtypeStruct((LANES // groups, heads), F32),
                jax.ShapeDtypeStruct((LANES // groups, LANES), F32),
            ),
            in_specs=[vmem] * 11,
            out_specs=[vmem] * 7,
            scratch_shapes=flat,
            compiler_params=pltpu.CompilerParams(
                collective_id=0, has_side_effects=True, vmem_limit_bytes=56 * 1024 * 1024
            ),
        )(
            node_feats[0], frame_blocks[0], src_ids, dst_ids, edge_bias[0],
            w_zero, w_one, w_two, alpha_w, out_proj, grad_out[0],
        )
        return (out[0][None], out[1][None], *out[2:])

    return run


def solution(mesh):
    placed = (
        P(("parts", "dp"), "graph", None),
        P(("parts", "dp"), ("graph", "sub"), None),
        P(("parts", "dp"), ("graph", "sub")),
        P(("parts", "dp"), ("graph", "sub")),
        P(("parts", "dp"), ("graph", "sub"), None),
        P(),
        P(),
        P(),
        P(),
        P(),
        P(("parts", "dp"), "graph", None),
    )
    graphs, dps = mesh.shape["graph"], mesh.shape["dp"]
    aligned = (128 // (graphs * 2)) % STEP == 0 and graphs >= 4 and mesh.shape["sub"] == 2
    return jax.shard_map(
        fused_body(graphs, dps, mesh.shape["parts"]) if aligned else body,
        mesh=mesh,
        in_specs=placed,
        out_specs=(
            P(("parts", "dp"), "graph", None),
            P(("parts", "dp"), ("graph", "sub"), None),
            P(("parts", "graph", "sub"), None),
            P("parts", ("graph", "sub"), None),
            P("parts", ("graph", "sub"), None),
            P(("parts", "graph", "sub"), None),
            P(("parts", "graph", "sub"), None),
        ),
        check_vma=False,
    )
```

```python
import jax
import jax.numpy as jnp
from jax import lax
from jax.experimental import pallas as pl
from jax.experimental.pallas import tpu as pltpu
from jax.sharding import PartitionSpec as P


def extended(block, sides, width):
    for axis, dim in sides:
        count = lax.axis_size(axis)
        forward = [(i, i + 1) for i in range(count - 1)]
        forward.append((count - 1, 0))
        backward = [(target, source) for source, target in forward]
        low = lax.ppermute(
            lax.slice_in_dim(block, block.shape[dim] - width, None, axis=dim), axis, forward
        )
        high = lax.ppermute(lax.slice_in_dim(block, 0, width, axis=dim), axis, backward)
        block = jnp.concatenate([low, block, high], axis=dim)
    return block


def combined_all(value, axis, join):
    pieces = jax.tree.map(lambda part: lax.all_gather(part, axis), value)
    head = jax.tree.map(lambda part: part[0], pieces)
    tail = jax.tree.map(lambda part: part[1:], pieces)
    running, _ = lax.scan(lambda running, section: (join(running, section), None), head, tail)
    return running


def passed_along(value, axis, by):
    peers = lax.axis_size(axis)
    return lax.ppermute(value, axis, [(i, (i + by) % peers) for i in range(peers)])


def contract(form, left, right):
    if left.dtype == right.dtype:
        return jnp.einsum(
            form, left, right, preferred_element_type=jnp.float32, precision=lax.Precision.HIGHEST
        )
    return jnp.einsum(form, left.astype(jnp.float32), right, precision=lax.Precision.HIGHEST)


def inner(left, right):
    return lax.dot_general(
        left, right, (((0,), (0,)), ((), ())), preferred_element_type=jnp.float32
    )


def across(left, right):
    return lax.dot_general(
        left, right, (((1,), (1,)), ((), ())), preferred_element_type=jnp.float32
    )


def frame_pieces(frames):
    pieces = []
    offset = 0
    for degree in range(5):
        breadth = 2 * degree + 1
        square = frames[:, offset : offset + breadth * breadth].reshape(-1, breadth, breadth)
        offset = offset + breadth * breadth
        reach = min(degree, 2)
        pieces.append(square[:, degree - reach : degree + reach + 1, :])
    return pieces


def degree_slice(matrix, degree, channels):
    return matrix[:, degree * degree * channels : (degree + 1) * (degree + 1) * channels].reshape(
        matrix.shape[0], 2 * degree + 1, channels
    )


def group_coeffs(pieces):
    centre = [min(degree, 2) for degree in range(5)]
    order_zero = jnp.concatenate(
        [pieces[degree][:, centre[degree], :] for degree in range(5)], axis=1
    )
    order_one = jnp.concatenate(
        [pieces[degree][:, centre[degree] + 1, :] for degree in range(1, 5)]
        + [pieces[degree][:, centre[degree] - 1, :] for degree in range(1, 5)],
        axis=1,
    )
    order_two = jnp.concatenate(
        [pieces[degree][:, 4, :] for degree in range(2, 5)]
        + [pieces[degree][:, 0, :] for degree in range(2, 5)],
        axis=1,
    )
    return (order_zero, order_one, order_two)


def split_coeffs(order_zero, order_one, order_two, breadth):
    pieces = []
    for degree in range(5):
        stacked = [order_zero[:, degree * breadth : (degree + 1) * breadth]]
        if degree >= 1:
            stacked = (
                [order_one[:, (3 + degree) * breadth : (4 + degree) * breadth]]
                + stacked
                + [order_one[:, (degree - 1) * breadth : degree * breadth]]
            )
        if degree >= 2:
            stacked = (
                [order_two[:, (1 + degree) * breadth : (2 + degree) * breadth]]
                + stacked
                + [order_two[:, (degree - 2) * breadth : (degree - 1) * breadth]]
            )
        pieces.append(jnp.stack(stacked, axis=1))
    return pieces


def pair_matrix(weights):
    real_part = weights[0]
    imag_part = weights[1]
    return jnp.concatenate(
        [
            jnp.concatenate([real_part, imag_part], axis=1),
            jnp.concatenate([-imag_part, real_part], axis=1),
        ],
        axis=0,
    )


def spread_heads(weights, value_ch):
    return jnp.repeat(weights, value_ch // weights.shape[1], axis=1)


def spread_rows(factor, value_ch):
    return jnp.tile(spread_heads(factor, value_ch), (1, 25))


def edge_forward(source_rows, pieces, w_zero, w_one, w_two, alpha_w, edge_bias):
    channels = source_rows.shape[1] // 25
    value_ch = w_zero.shape[1] // 5
    rotated = [
        contract(
            "ekm,emc->ekc", pieces[degree], degree_slice(source_rows, degree, channels)
        ).astype(jnp.bfloat16)
        for degree in range(5)
    ]
    inputs = group_coeffs(rotated)
    out_zero = jnp.dot(inputs[0], w_zero, preferred_element_type=jnp.float32)
    out_one = jnp.dot(inputs[1], pair_matrix(w_one), preferred_element_type=jnp.float32)
    out_two = jnp.dot(inputs[2], pair_matrix(w_two), preferred_element_type=jnp.float32)
    scalar = out_zero[:, :value_ch]
    gate = jax.nn.silu(scalar).astype(jnp.bfloat16)
    logits = jnp.dot(gate, alpha_w, preferred_element_type=jnp.float32) + edge_bias
    values = split_coeffs(
        out_zero.astype(jnp.bfloat16),
        out_one.astype(jnp.bfloat16),
        out_two.astype(jnp.bfloat16),
        value_ch,
    )
    return (inputs, scalar, gate, logits, values)


def rotate_back(weights, values, pieces):
    value_ch = values[0].shape[2]
    spread = spread_heads(weights, value_ch)[:, None, :]
    outputs = [
        contract("ekm,ekv->emv", pieces[degree], values[degree].astype(jnp.float32) * spread)
        for degree in range(5)
    ]
    return jnp.concatenate([item.reshape(item.shape[0], -1) for item in outputs], axis=1)


def attention_grads(grad_back, values, pieces, heads):
    value_ch = values[0].shape[2]
    message_grads = [
        contract("ekm,emv->ekv", pieces[degree], degree_slice(grad_back, degree, value_ch))
        for degree in range(5)
    ]
    product = jnp.sum(message_grads[0] * values[0].astype(jnp.float32), axis=1)
    for degree in range(1, 5):
        product = product + jnp.sum(
            message_grads[degree] * values[degree].astype(jnp.float32), axis=1
        )
    head_grad = product.reshape(product.shape[0], heads, value_ch // heads).sum(axis=2)
    return (message_grads, head_grad)


def value_grads(message_grads, attention, logit_grad, scalar, alpha_w):
    value_ch = scalar.shape[1]
    spread = spread_heads(attention, value_ch)[:, None, :]
    grads = [item * spread for item in message_grads]
    order_zero, order_one, order_two = group_coeffs(grads)
    sigmoid = jax.nn.sigmoid(scalar)
    gate_grad = across(logit_grad, alpha_w) * sigmoid * (1.0 + scalar * (1.0 - sigmoid))
    order_zero = jnp.concatenate(
        [order_zero[:, :value_ch] + gate_grad, order_zero[:, value_ch:]], axis=1
    )
    return (
        order_zero.astype(jnp.bfloat16),
        order_one.astype(jnp.bfloat16),
        order_two.astype(jnp.bfloat16),
    )


def pair_grad(block, half_in, half_out):
    return jnp.stack(
        [
            block[:half_in, :half_out] + block[half_in:, half_out:],
            block[:half_in, half_out:] - block[half_in:, :half_out],
        ]
    )


def input_grads(inputs, grads, w_zero, w_one, w_two, pieces, channels):
    weight_zero = inner(inputs[0], grads[0])
    weight_one = pair_grad(inner(inputs[1], grads[1]), w_one.shape[1], w_one.shape[2])
    weight_two = pair_grad(inner(inputs[2], grads[2]), w_two.shape[1], w_two.shape[2])
    coeff_zero = across(grads[0], w_zero).astype(jnp.bfloat16)
    coeff_one = across(grads[1], pair_matrix(w_one)).astype(jnp.bfloat16)
    coeff_two = across(grads[2], pair_matrix(w_two)).astype(jnp.bfloat16)
    coeff_pieces = split_coeffs(coeff_zero, coeff_one, coeff_two, channels)
    row_grads = jnp.concatenate(
        [
            contract("ekm,ekc->emc", pieces[degree], coeff_pieces[degree]).reshape(
                coeff_zero.shape[0], -1
            )
            for degree in range(5)
        ],
        axis=1,
    )
    return ((weight_zero, weight_one, weight_two), row_grads)


def grouped_rows(item, groups):
    if item.ndim == 3:
        return jnp.transpose(
            item.reshape(2, groups, item.shape[1] // groups, item.shape[2]), (1, 0, 2, 3)
        ).reshape(groups, -1)
    return item.reshape(groups, -1)


def body(
    node_feats,
    frame_blocks,
    src_ids,
    dst_ids,
    edge_bias,
    w_zero,
    w_one,
    w_two,
    alpha_w,
    out_proj,
    grad_out,
):
    tile_rows = node_feats.shape[1]
    channels = node_feats.shape[2] // 25
    value_ch = w_zero.shape[1] // 5
    heads = alpha_w.shape[1]
    owners = lax.axis_size("graph")
    owner = lax.axis_index("graph")
    padded = extended(node_feats, (("graph", 1),), tile_rows)[0]
    sources = src_ids[0]
    targets = dst_ids[0] - owner * tile_rows
    slots = (sources // tile_rows - owner + 1 + owners) % owners * tile_rows + sources % tile_rows
    pieces = frame_pieces(frame_blocks[0])
    source_rows = jnp.take(padded, slots, axis=0)
    inputs, scalar, gate, logits, values = edge_forward(
        source_rows, pieces, w_zero, w_one, w_two, alpha_w, edge_bias[0]
    )
    local_max = jnp.maximum(
        jax.ops.segment_max(logits, targets, num_segments=tile_rows, indices_are_sorted=True), -1e30
    )
    raised = jnp.exp(logits - local_max[targets])
    local_total = jax.ops.segment_sum(
        raised, targets, num_segments=tile_rows, indices_are_sorted=True
    )
    local_acc = jax.ops.segment_sum(
        rotate_back(raised, values, pieces),
        targets,
        num_segments=tile_rows,
        indices_are_sorted=True,
    )

    def combine(earlier, later):
        highest = jnp.maximum(earlier[0], later[0])
        left_scale = jnp.exp(earlier[0] - highest)
        right_scale = jnp.exp(later[0] - highest)
        return (
            highest,
            earlier[1] * left_scale + later[1] * right_scale,
            earlier[2] * spread_rows(left_scale, value_ch)
            + later[2] * spread_rows(right_scale, value_ch),
        )

    highest, totals, summed = combined_all((local_max, local_total, local_acc), "sub", combine)
    summed_half = (summed / spread_rows(totals, value_ch)).astype(jnp.bfloat16)
    attention = jnp.exp(logits - highest[targets]) / totals[targets]
    own_rows = node_feats[0]
    projected = jnp.dot(
        summed_half.reshape(-1, value_ch), out_proj, preferred_element_type=jnp.float32
    ).reshape(tile_rows, -1)
    updated = (own_rows.astype(jnp.float32) + projected).astype(jnp.bfloat16)
    own_grad = grad_out[0]
    half_rows = tile_rows // lax.axis_size("sub")
    half_start = lax.axis_index("sub") * half_rows
    summed_share = lax.dynamic_slice_in_dim(summed_half, half_start, half_rows, 0)
    grad_share = lax.dynamic_slice_in_dim(own_grad, half_start, half_rows, 0)
    proj_grad = inner(summed_share.reshape(-1, value_ch), grad_share.reshape(-1, channels))
    summed_grad = across(own_grad.reshape(-1, channels), out_proj).reshape(tile_rows, -1)
    message_grads, head_grad = attention_grads(summed_grad[targets], values, pieces, heads)
    local_dots = jax.ops.segment_sum(
        attention * head_grad, targets, num_segments=tile_rows, indices_are_sorted=True
    )
    dots = lax.psum(local_dots, "sub")
    logit_grad = (attention * (head_grad - dots[targets])).astype(jnp.bfloat16)
    alpha_grad = inner(gate, logit_grad)
    grads = value_grads(message_grads, attention, logit_grad, scalar, alpha_w)
    conv_grads, row_grads = input_grads(inputs, grads, w_zero, w_one, w_two, pieces, channels)
    buffer_grads = jax.ops.segment_sum(row_grads, slots, num_segments=3 * tile_rows)
    from_after = passed_along(buffer_grads[:tile_rows].astype(jnp.bfloat16), "graph", -1).astype(
        jnp.float32
    )
    from_before = passed_along(
        buffer_grads[2 * tile_rows :].astype(jnp.bfloat16), "graph", 1
    ).astype(jnp.float32)
    own_total = buffer_grads[tile_rows : 2 * tile_rows] + from_after + from_before
    node_share = lax.psum_scatter(
        own_total.astype(jnp.bfloat16), "sub", scatter_dimension=0, tiled=True
    ).astype(jnp.float32)
    grad_nodes = node_share + grad_share.astype(jnp.float32)
    terms = conv_grads + (alpha_grad, proj_grad)
    groups = lax.axis_size("graph") * lax.axis_size("sub")
    flattened = jnp.concatenate([grouped_rows(item, groups) for item in terms], axis=1)
    share = lax.psum_scatter(
        flattened.astype(jnp.bfloat16), ("graph", "sub"), scatter_dimension=0, tiled=True
    ).astype(jnp.float32)
    share = lax.psum(share.astype(jnp.bfloat16), "dp").astype(jnp.float32)[0]
    results = []
    offset = 0
    for item in terms:
        count = item.size // groups
        piece = share[offset : offset + count]
        if item.ndim == 3:
            results.append(piece.reshape(2, item.shape[1] // groups, item.shape[2]))
        else:
            results.append(piece.reshape(item.shape[0] // groups, item.shape[1]))
        offset = offset + count
    return (
        updated[None],
        grad_nodes[None],
        results[0],
        results[1],
        results[2],
        results[3],
        results[4],
    )


def column(degree, order):
    if order == 0:
        return degree
    if order == 1:
        return 5 + degree - 1
    if order == -1:
        return 9 + degree - 1
    if order == 2:
        return 13 + degree - 2
    return 16 + degree - 2


def frame_entries():
    entries = []
    offset = 0
    for degree in range(5):
        breadth = 2 * degree + 1
        reach = min(degree, 2)
        for order in range(-reach, reach + 1):
            for full in range(breadth):
                entries.append((degree, order, full, offset + (degree + order) * breadth + full))
        offset += breadth * breadth
    return entries


ENTRIES = frame_entries()
INDEX = {(d, o, f): i for i, (d, o, f, _) in enumerate(ENTRIES)}
LANES = 128
STEP = 16
F32 = jnp.float32
BF16 = jnp.bfloat16


def exact(left, right):
    return jnp.dot(left, right, preferred_element_type=F32, precision=lax.Precision.HIGHEST)


def fast(left, right):
    return jnp.dot(left, right, preferred_element_type=F32)


def lanes(index, count=1):
    return slice(index * LANES, (index + count) * LANES)


def fused(
    graphs, dps, parts,
    nf, fr, src, dst, bias, w0_in, w1_in, w2_in, aw, op, go,
    upd, gn, tiles_out,
    w0, w1, w2,
    halo, small, small_in, acc_out, acc_in, fb, gp, sr, mg, zz, vv, weight, bk, gg, ig, rg, ng, ng_in,
    wg, r1, hh, r2, kk, r3, fin,
    load_sem, halo_send, halo_recv, small_send, small_recv, acc_send, acc_recv, ng_send, ng_recv,
    s1s, s1r, s2s, s2r, s3s, s3r, s4s, s4r,
):
    edges = fr.shape[0]
    rows_dev = nf.shape[0]
    heads = aw.shape[0]
    g = lax.axis_index("graph")
    s = lax.axis_index("sub")
    d = lax.axis_index("dp")
    other = 1 - s

    def along(k):
        return lax.rem(g + k + graphs, graphs)

    def dp_along(k):
        return lax.rem(d + k, dps)

    def remote(source, target, send, recv, device):
        return pltpu.make_async_remote_copy(
            src_ref=source, dst_ref=target, send_sem=send, recv_sem=recv,
            device_id=device, device_id_type=pl.DeviceIdType.MESH,
        )

    loads = [
        pltpu.make_async_copy(source, target, load_sem.at[i])
        for i, (source, target) in enumerate(((w0_in, w0), (w1_in, w1), (w2_in, w2)))
    ]
    for load in loads:
        load.start()

    barrier = pltpu.get_barrier_semaphore()
    peers = [{"sub": other}]
    for k in range(1, graphs):
        peers.append({"graph": along(k)})
    peers.append({"graph": along(1), "sub": other})
    peers.append({"graph": along(-1), "sub": other})
    for k in range(1, dps):
        peers.append({"dp": dp_along(k)})
    for peer in peers:
        pl.semaphore_signal(barrier, inc=1, device_id=peer, device_id_type=pl.DeviceIdType.MESH)
    pl.semaphore_wait(barrier, len(peers))

    halo_up = remote(nf, halo.at[0], halo_send.at[0], halo_recv.at[0], {"graph": along(1)})
    halo_down = remote(nf, halo.at[1], halo_send.at[1], halo_recv.at[1], {"graph": along(-1)})
    halo_up.start()
    halo_down.start()

    src_row = src[...]
    dst_row = dst[...]
    eye = lax.broadcasted_iota(jnp.int32, (edges, edges), 0) == lax.broadcasted_iota(
        jnp.int32, (edges, edges), 1
    )

    def to_column(row):
        spread = jnp.where(eye, jnp.broadcast_to(row.astype(F32), (edges, edges)), 0.0)
        return jnp.sum(spread, axis=1, keepdims=True).astype(jnp.int32)

    src_col = to_column(src_row)
    dst_col = to_column(dst_row) - g * rows_dev
    lane48 = lax.broadcasted_iota(jnp.int32, (edges, 3 * rows_dev), 1)
    row48 = lax.broadcasted_iota(jnp.int32, (3 * rows_dev, edges), 0)

    def block_ids(position):
        low = along(-1) * rows_dev + position
        mid = g * rows_dev + position - rows_dev
        high = along(1) * rows_dev + position - 2 * rows_dev
        return jnp.where(
            position < rows_dev, low, jnp.where(position < 2 * rows_dev, mid, high)
        )

    def hot(match, dtype=BF16):
        return jnp.where(match, 1.0, 0.0).astype(dtype)

    pick_src = hot(block_ids(lane48) == src_col)
    put_src = hot(block_ids(row48) == src_row)
    pick_dst = hot(lax.broadcasted_iota(jnp.int32, (edges, rows_dev), 1) == dst_col)
    put_dst = hot(
        lax.broadcasted_iota(jnp.int32, (rows_dev, edges), 0) == dst_row - g * rows_dev
    )
    lane_j = lax.broadcasted_iota(jnp.int32, (edges, LANES), 1)
    mine = lax.shift_right_logical(lane_j, 3) == dst_col
    sq0 = lax.broadcasted_iota(jnp.int32, (LANES, LANES), 0)
    sq1 = lax.broadcasted_iota(jnp.int32, (LANES, LANES), 1)
    spread = hot(jnp.bitwise_and(sq0, 7) == lax.shift_right_logical(sq1, 4), F32)
    gather_heads = hot(lax.shift_right_logical(sq0, 4) == jnp.bitwise_and(sq1, 7), F32)
    compact = hot(jnp.bitwise_and(sq0, 7) == sq1)
    tile_heads = hot(
        lax.broadcasted_iota(jnp.int32, (heads, LANES), 0)
        == jnp.bitwise_and(lax.broadcasted_iota(jnp.int32, (heads, LANES), 1), 7),
        F32,
    )
    alpha_t = inner(aw[...], tile_heads.astype(BF16)).astype(BF16)
    proj = op[...]

    for k in range(25):
        rows = fast(pick_dst, go[:, lanes(k)]).astype(BF16)
        gp[:, lanes(k)] = across(rows, proj)

    def message_step(c, _):
        at = pl.ds(pl.multiple_of(c * STEP, STEP), STEP)
        frames = fr[at, :].astype(F32)
        for degree in range(5):
            reach = min(degree, 2)
            breadth = 2 * degree + 1
            inputs = [gp[at, lanes(degree * degree + f)] for f in range(breadth)]
            for order in range(-reach, reach + 1):
                total = None
                for f in range(breadth):
                    i = INDEX[(degree, order, f)]
                    col = ENTRIES[i][3]
                    value = jnp.broadcast_to(frames[:, col : col + 1], (STEP, LANES))
                    fb[i, at, :] = value
                    term = value * inputs[f]
                    total = term if total is None else total + term
                mg[at, lanes(column(degree, order))] = total
        return 0

    lax.fori_loop(0, edges // STEP, message_step, 0)

    halo_up.wait()
    halo_down.wait()
    for k in range(25):
        block = jnp.concatenate([halo[0, :, lanes(k)], nf[:, lanes(k)], halo[1, :, lanes(k)]], axis=0)
        sr[:, lanes(k)] = fast(pick_src, block)

    def rotate_step(c, _):
        at = pl.ds(pl.multiple_of(c * STEP, STEP), STEP)
        for degree in range(5):
            reach = min(degree, 2)
            breadth = 2 * degree + 1
            inputs = [sr[at, lanes(degree * degree + f)] for f in range(breadth)]
            for order in range(-reach, reach + 1):
                total = None
                for f in range(breadth):
                    term = fb[INDEX[(degree, order, f)], at, :] * inputs[f]
                    total = term if total is None else total + term
                zz[at, lanes(column(degree, order))] = total.astype(BF16)
        return 0

    lax.fori_loop(0, edges // STEP, rotate_step, 0)

    for load in loads:
        load.wait()
    z0 = zz[:, lanes(0, 5)]
    zp1, zm1 = zz[:, lanes(5, 4)], zz[:, lanes(9, 4)]
    zp2, zm2 = zz[:, lanes(13, 3)], zz[:, lanes(16, 3)]
    y0 = fast(z0, w0[...])
    scalar = y0[:, :LANES]
    vv[:, lanes(0, 5)] = y0.astype(BF16)
    vv[:, lanes(5, 4)] = (fast(zp1, w1[0]) - fast(zm1, w1[1])).astype(BF16)
    vv[:, lanes(9, 4)] = (fast(zp1, w1[1]) + fast(zm1, w1[0])).astype(BF16)
    vv[:, lanes(13, 3)] = (fast(zp2, w2[0]) - fast(zm2, w2[1])).astype(BF16)
    vv[:, lanes(16, 3)] = (fast(zp2, w2[1]) + fast(zm2, w2[0])).astype(BF16)
    bias_lanes = lax.dot_general(
        bias[...], tile_heads, (((0,), (0,)), ((), ())),
        preferred_element_type=F32, precision=lax.Precision.HIGHEST,
    )
    sigmoid = lax.logistic(scalar)
    gate = (scalar * sigmoid).astype(BF16)
    logits = fast(gate, alpha_t) + bias_lanes
    logits = jnp.where(mine, logits, -1e30)
    product = None
    for k in range(19):
        term = mg[:, lanes(k)] * vv[:, lanes(k)].astype(F32)
        product = term if product is None else product + term
    head_grad = exact(product, gather_heads)
    peak = jnp.max(logits, axis=0, keepdims=True)
    raised = jnp.where(mine, jnp.exp(logits - peak), 0.0)
    total = jnp.sum(raised, axis=0, keepdims=True)
    dots = jnp.sum(raised * head_grad, axis=0, keepdims=True)
    small[0:1, :] = peak
    small[1:2, :] = total
    small[2:3, :] = dots
    small[3:8, :] = jnp.zeros((5, LANES), F32)
    small_copy = remote(small, small_in, small_send, small_recv, {"sub": other})
    small_copy.start()

    weight[...] = exact(raised, spread)

    def back_step(c, _):
        at = pl.ds(pl.multiple_of(c * STEP, STEP), STEP)
        scale = weight[at, :]
        for degree in range(5):
            reach = min(degree, 2)
            orders = range(-reach, reach + 1)
            inputs = {o: vv[at, lanes(column(degree, o))].astype(F32) * scale for o in orders}
            for f in range(2 * degree + 1):
                out = None
                for o in orders:
                    term = fb[INDEX[(degree, o, f)], at, :] * inputs[o]
                    out = term if out is None else out + term
                bk[at, lanes(degree * degree + f)] = out.astype(BF16)
        return 0

    lax.fori_loop(0, edges // STEP, back_step, 0)
    small_copy.wait()
    peak_in = small_in[0:1, :]
    top = jnp.maximum(peak, peak_in)
    own_scale = jnp.exp(peak - top)
    in_scale = jnp.exp(peak_in - top)
    whole = total * own_scale + small_in[1:2, :] * in_scale
    all_dots = (dots * own_scale + small_in[2:3, :] * in_scale) / whole
    node_lane = lax.broadcasted_iota(jnp.int32, (rows_dev, LANES), 1)
    node_row = lax.broadcasted_iota(jnp.int32, (rows_dev, LANES), 0)
    node_scale = exact(
        jnp.where(lax.shift_right_logical(node_lane, 3) == node_row, own_scale / whole, 0.0), spread
    )
    for k in range(25):
        acc_out[:, lanes(k)] = fast(put_dst, bk[:, lanes(k)]) * node_scale
    acc_copy = remote(acc_out, acc_in, acc_send, acc_recv, {"sub": other})
    acc_copy.start()

    attention = raised * (own_scale / whole)
    logit_grad = (attention * (head_grad - all_dots)).astype(BF16)
    spread_att = exact(attention, spread)
    gate_grad = across(logit_grad, alpha_t) * sigmoid * (1.0 + scalar * (1.0 - sigmoid))
    for k in range(19):
        grad = mg[:, lanes(k)] * spread_att
        if k == 0:
            grad = grad + gate_grad
        gg[:, lanes(k)] = grad.astype(BF16)

    groups = graphs * 2

    def put(piece, base, rows_share, row0, matrix):
        wide = matrix.shape[1] // LANES
        part = wg[piece].shape[3]
        for i in range(matrix.shape[0] // STEP):
            row = row0 + i * STEP
            group = row // rows_share
            inner_row = (row % rows_share) // STEP
            for j in range(wide):
                tile = base + inner_row * wide + j
                wg[piece][group % 2, tile // part, group // 2, tile % part] = matrix[
                    i * STEP : (i + 1) * STEP, lanes(j)
                ].astype(BF16)

    def zero_tail(piece, used):
        part = wg[piece].shape[3]
        for tile in range(used, part * dps):
            wg[piece][:, tile // part, :, tile % part] = jnp.zeros((2, graphs, STEP, LANES), BF16)

    def stage_one(piece):
        return remote(
            wg[piece].at[other], r1[piece], s1s.at[piece], s1r.at[piece], {"sub": other}
        )

    def stage_two(piece):
        return [
            remote(
                hh[piece].at[dp_along(k)], r2[piece].at[k - 1],
                s2s.at[piece, k - 1], s2r.at[piece, k - 1], {"dp": dp_along(k)},
            )
            for k in range(1, dps)
        ]

    def stage_three(piece):
        return [
            remote(
                kk[piece].at[along(k)], r3[piece].at[k - 1],
                s3s.at[piece, k - 1], s3r.at[piece, k - 1], {"graph": along(k)},
            )
            for k in range(1, graphs)
        ]

    def stage_four(piece):
        return [
            remote(
                fin[piece].at[0], fin[piece].at[k],
                s4s.at[piece, k - 1], s4r.at[piece, k - 1], {"dp": dp_along(k)},
            )
            for k in range(1, dps)
        ]

    def start(copies):
        for copy in copies:
            copy.start()
        return copies

    def wait(copies):
        for copy in copies:
            copy.wait()

    gp1, gm1 = gg[:, lanes(5, 4)], gg[:, lanes(9, 4)]
    rows1 = 512 // groups
    one = [None] * 4
    tiles1 = (rows1 // STEP) * 4
    for b in range(4):
        put(0, 0, rows1, b * LANES, inner(zz[:, lanes(5 + b)], gp1) + inner(zz[:, lanes(9 + b)], gm1))
    zero_tail(0, tiles1)
    one[0] = stage_one(0)
    one[0].start()
    for b in range(4):
        put(1, 0, rows1, b * LANES, inner(zz[:, lanes(5 + b)], gm1) - inner(zz[:, lanes(9 + b)], gp1))
    zero_tail(1, tiles1)
    one[1] = stage_one(1)
    one[1].start()

    g0 = gg[:, lanes(0, 5)]
    rows0 = 640 // groups
    for b in range(5):
        put(2, 0, rows0, b * LANES, inner(zz[:, lanes(b)], g0))
    alpha_rows = LANES // groups
    tiles0 = (rows0 // STEP) * 5
    logit_small = fast(logit_grad, compact).astype(BF16)
    put(2, tiles0, alpha_rows, 0, inner(gate, logit_small))
    zero_tail(2, tiles0 + alpha_rows // STEP)
    one[2] = stage_one(2)
    one[2].start()

    def add_one(piece):
        one[piece].wait()
        for p in range(dps):
            hh[piece][p] = wg[piece][s, p] + r1[piece][p]
        return start(stage_two(piece))

    def add_two(piece):
        wait(two[piece])
        if dps == 2:
            kk[piece][...] = hh[piece][d] + r2[piece][0]
        else:
            value = hh[piece][d].astype(F32)
            for k in range(1, dps):
                value = value + r2[piece][k - 1].astype(F32)
            kk[piece][...] = value.astype(BF16)
        return start(stage_three(piece))

    def add_three(piece):
        wait(three[piece])
        value = kk[piece][g].astype(F32)
        for k in range(1, graphs):
            value = value + r3[piece][k - 1].astype(F32)
        fin[piece][0] = value.astype(BF16)
        return start(stage_four(piece))

    two = [None] * 4
    three = [None] * 4
    four = [None] * 4
    two[0] = add_one(0)

    acc_copy.wait()
    summed = jnp.concatenate(
        [(acc_out[:, lanes(k)] + acc_in[:, lanes(k)]).astype(BF16) for k in range(25)], axis=0
    )
    cotangent = jnp.concatenate([go[:, lanes(k)] for k in range(25)], axis=0)
    half = rows_dev // 2
    in_half = lax.broadcasted_iota(jnp.int32, summed.shape, 0)
    in_half = lax.shift_right_logical(jnp.bitwise_and(in_half, rows_dev - 1), 3) == s
    share = jnp.where(in_half, summed.astype(F32), 0.0).astype(BF16)
    gp2, gm2 = gg[:, lanes(13, 3)], gg[:, lanes(16, 3)]
    rows2 = 384 // groups
    tiles2 = (rows2 // STEP) * 3
    for b in range(3):
        zp, zm = zz[:, lanes(13 + b)], zz[:, lanes(16 + b)]
        put(3, 0, rows2, b * LANES, inner(zp, gp2) + inner(zm, gm2))
        put(3, tiles2, rows2, b * LANES, inner(zp, gm2) - inner(zm, gp2))
    put(3, 2 * tiles2, alpha_rows, 0, inner(share, cotangent))
    zero_tail(3, 2 * tiles2 + alpha_rows // STEP)
    one[3] = stage_one(3)
    one[3].start()
    two[1] = add_one(1)

    ig[:, lanes(0, 5)] = across(g0, w0[...]).astype(BF16)
    ig[:, lanes(5, 4)] = (across(gp1, w1[0]) + across(gm1, w1[1])).astype(BF16)
    two[2] = add_one(2)
    ig[:, lanes(9, 4)] = (across(gm1, w1[0]) - across(gp1, w1[1])).astype(BF16)
    ig[:, lanes(13, 3)] = (across(gp2, w2[0]) + across(gm2, w2[1])).astype(BF16)
    ig[:, lanes(16, 3)] = (across(gm2, w2[0]) - across(gp2, w2[1])).astype(BF16)
    two[3] = add_one(3)

    def row_step(c, _):
        at = pl.ds(pl.multiple_of(c * STEP, STEP), STEP)
        for degree in range(5):
            reach = min(degree, 2)
            orders = range(-reach, reach + 1)
            inputs = {o: ig[at, lanes(column(degree, o))].astype(F32) for o in orders}
            for f in range(2 * degree + 1):
                out = None
                for o in orders:
                    term = fb[INDEX[(degree, o, f)], at, :] * inputs[o]
                    out = term if out is None else out + term
                rg[at, lanes(degree * degree + f)] = out.astype(BF16)
        return 0

    lax.fori_loop(0, edges // STEP, row_step, 0)

    for k in range(13):
        low = fast(put_src, rg[:, lanes(k)])
        high = fast(put_src, rg[:, lanes(13 + k)]) if k < 12 else jnp.zeros_like(low)
        for b in range(3):
            for h in range(2):
                at = slice(b * rows_dev + h * half, b * rows_dev + (h + 1) * half)
                ng[b, h, :, lanes(k)] = jnp.concatenate([low[at], high[at]], axis=0).astype(BF16)
    node_copies = []
    for b in range(3):
        for r in range(2):
            if b == 1 and r == 0:
                continue
            to = lax.rem(s + r, 2)
            node_copies.append(
                remote(
                    ng.at[b, to], ng_in.at[b, r], ng_send.at[b, r], ng_recv.at[b, r],
                    {"graph": along(b - 1), "sub": to},
                )
            )
    start(node_copies)

    three[0] = add_two(0)
    three[1] = add_two(1)

    projected = fast(summed, proj)
    for k in range(25):
        upd[:, lanes(k)] = (
            nf[:, lanes(k)].astype(F32) + projected[k * rows_dev : (k + 1) * rows_dev]
        ).astype(BF16)
    three[2] = add_two(2)

    wait(node_copies)
    for k in range(13):
        value = ng[1, s, :, lanes(k)].astype(F32)
        for b in range(3):
            for r in range(2):
                if b == 1 and r == 0:
                    continue
                value = value + ng_in[b, r, :, lanes(k)].astype(F32)
        for part, coef in ((0, k), (1, 13 + k)):
            if coef < 25:
                base = go[:, lanes(coef)].astype(F32)
                base = jnp.where(s == 0, base[:half], base[half:])
                gn[:, lanes(coef)] = value[part * half : (part + 1) * half] + base

    three[3] = add_two(3)
    for piece in range(4):
        four[piece] = add_three(piece)
    base = 0
    for piece, count in enumerate(
        (tiles1, tiles1, tiles0 + alpha_rows // STEP, 2 * tiles2 + alpha_rows // STEP)
    ):
        wait(four[piece])
        part = fin[piece].shape[1]
        for p in range(dps):
            size = min(part, count - p * part)
            if size > 0:
                at = base + p * part
                tiles_out[at : at + size] = fin[piece][lax.rem(d - p + dps, dps), :size]
        base += count


def unpack(upd, gn, tiles, upd_out, gn_out, o0, o1, o2, oa, oproj):
    upd_out[...] = upd[...]
    gn_out[...] = gn[...]
    base = 0

    def matrix(write, rows, wide):
        nonlocal base
        for i in range(rows // STEP):
            for j in range(wide):
                write(slice(i * STEP, (i + 1) * STEP), lanes(j), tiles[base].astype(F32))
                base += 1

    def into(ref, lead=None):
        def write(rows, columns, value):
            if lead is None:
                ref[rows, columns] = value
            else:
                ref[lead, rows, columns] = value

        return write

    for q in range(2):
        matrix(into(o1, q), o1.shape[1], 4)
    matrix(into(o0), o0.shape[0], 5)
    for i in range(oa.shape[1] // STEP):
        pick = lax.broadcasted_iota(jnp.int32, (oa.shape[0], LANES), 0) == lax.broadcasted_iota(
            jnp.int32, (oa.shape[0], LANES), 1
        )
        oa[:, i * STEP : (i + 1) * STEP] = across(
            jnp.where(pick, 1.0, 0.0).astype(BF16), tiles[base]
        )
        base += 1
    for q in range(2):
        matrix(into(o2, q), o2.shape[1], 3)
    matrix(into(oproj), oproj.shape[0], 1)


def fused_body(graphs, dps, parts):
    groups = graphs * 2

    def run(node_feats, frame_blocks, src_ids, dst_ids, edge_bias, w_zero, w_one, w_two, alpha_w, out_proj, grad_out):
        rows_dev = node_feats.shape[1]
        edges = frame_blocks.shape[1]
        heads = alpha_w.shape[1]
        used = (
            (512 // groups // STEP) * 4,
            (512 // groups // STEP) * 4,
            (640 // groups // STEP) * 5 + LANES // groups // STEP,
            2 * (384 // groups // STEP) * 3 + LANES // groups // STEP,
        )
        part = [-(-count // dps) for count in used]
        dma = pltpu.SemaphoreType.DMA
        wide = 25 * LANES
        kept = 19 * LANES

        def per_piece(lead):
            return [pltpu.VMEM((*lead(p), STEP, LANES), BF16) for p in part]

        scratch = [
            pltpu.VMEM(w_zero.shape, BF16),
            pltpu.VMEM(w_one.shape, BF16),
            pltpu.VMEM(w_two.shape, BF16),
            pltpu.VMEM((2, rows_dev, wide), BF16),
            pltpu.VMEM((8, LANES), F32),
            pltpu.VMEM((8, LANES), F32),
            pltpu.VMEM((rows_dev, wide), F32),
            pltpu.VMEM((rows_dev, wide), F32),
            pltpu.VMEM((len(ENTRIES), edges, LANES), F32),
            pltpu.VMEM((edges, wide), F32),
            pltpu.VMEM((edges, wide), F32),
            pltpu.VMEM((edges, kept), F32),
            pltpu.VMEM((edges, kept), BF16),
            pltpu.VMEM((edges, kept), BF16),
            pltpu.VMEM((edges, LANES), F32),
            pltpu.VMEM((edges, wide), BF16),
            pltpu.VMEM((edges, kept), BF16),
            pltpu.VMEM((edges, kept), BF16),
            pltpu.VMEM((edges, wide), BF16),
            pltpu.VMEM((3, 2, STEP, 13 * LANES), BF16),
            pltpu.VMEM((3, 2, STEP, 13 * LANES), BF16),
            per_piece(lambda p: (2, dps, graphs, p)),
            per_piece(lambda p: (dps, graphs, p)),
            per_piece(lambda p: (dps, graphs, p)),
            per_piece(lambda p: (max(dps - 1, 1), graphs, p)),
            per_piece(lambda p: (graphs, p)),
            per_piece(lambda p: (graphs - 1, p)),
            per_piece(lambda p: (dps, p)),
            dma((3,)), dma((2,)), dma((2,)), dma, dma, dma, dma, dma((3, 2)), dma((3, 2)),
            dma((4,)), dma((4,)),
            dma((4, max(dps - 1, 1))), dma((4, max(dps - 1, 1))),
            dma((4, graphs - 1)), dma((4, graphs - 1)),
            dma((4, max(dps - 1, 1))), dma((4, max(dps - 1, 1))),
        ]
        flat = []
        counts = []
        for item in scratch:
            if isinstance(item, list):
                counts.append(len(item))
                flat.extend(item)
            else:
                counts.append(0)
                flat.append(item)

        def entry(*refs):
            lead, rest = refs[:14], list(refs[14:])
            grouped = []
            for count in counts:
                if count:
                    grouped.append(rest[:count])
                    rest = rest[count:]
                else:
                    grouped.append(rest.pop(0))
            fused(graphs, dps, parts, *lead, *grouped)

        vmem = pl.BlockSpec(memory_space=pltpu.VMEM)
        anywhere = pl.BlockSpec(memory_space=pl.ANY)
        count = sum(used)
        packed = pl.pallas_call(
            entry,
            out_shape=(
                jax.ShapeDtypeStruct((rows_dev, wide), BF16),
                jax.ShapeDtypeStruct((rows_dev // 2, wide), F32),
                jax.ShapeDtypeStruct((count, STEP, LANES), BF16),
            ),
            in_specs=[vmem] * 5 + [anywhere] * 3 + [vmem] * 3,
            out_specs=[vmem] * 3,
            scratch_shapes=flat,
            compiler_params=pltpu.CompilerParams(
                collective_id=0, has_side_effects=True, vmem_limit_bytes=56 * 1024 * 1024
            ),
        )(
            node_feats[0], frame_blocks[0], src_ids, dst_ids, edge_bias[0].T,
            w_zero, w_one, w_two, alpha_w.T, out_proj, grad_out[0],
        )
        out = pl.pallas_call(
            unpack,
            out_shape=(
                jax.ShapeDtypeStruct((rows_dev, wide), BF16),
                jax.ShapeDtypeStruct((rows_dev // 2, wide), F32),
                jax.ShapeDtypeStruct((640 // groups, 640), F32),
                jax.ShapeDtypeStruct((2, 512 // groups, 512), F32),
                jax.ShapeDtypeStruct((2, 384 // groups, 384), F32),
                jax.ShapeDtypeStruct((heads, LANES // groups), F32),
                jax.ShapeDtypeStruct((LANES // groups, LANES), F32),
            ),
            in_specs=[vmem] * 3,
            out_specs=[vmem] * 7,
        )(*packed)
        return (out[0][None], out[1][None], out[2], out[3], out[4], out[5].T, out[6])

    return run


def solution(mesh):
    placed = (
        P(("parts", "dp"), "graph", None),
        P(("parts", "dp"), ("graph", "sub"), None),
        P(("parts", "dp"), ("graph", "sub")),
        P(("parts", "dp"), ("graph", "sub")),
        P(("parts", "dp"), ("graph", "sub"), None),
        P(),
        P(),
        P(),
        P(),
        P(),
        P(("parts", "dp"), "graph", None),
    )
    graphs, dps = mesh.shape["graph"], mesh.shape["dp"]
    aligned = (128 // (graphs * 2)) % STEP == 0 and graphs >= 4 and mesh.shape["sub"] == 2
    return jax.shard_map(
        fused_body(graphs, dps, mesh.shape["parts"]) if aligned else body,
        mesh=mesh,
        in_specs=placed,
        out_specs=(
            P(("parts", "dp"), "graph", None),
            P(("parts", "dp"), ("graph", "sub"), None),
            P(("parts", "graph", "sub"), None),
            P("parts", ("graph", "sub"), None),
            P("parts", ("graph", "sub"), None),
            P(("parts", "graph", "sub"), None),
            P(("parts", "graph", "sub"), None),
        ),
        check_vma=False,
    )
```

```python
import jax
import jax.numpy as jnp
from jax import lax
from jax.experimental import pallas as pl
from jax.experimental.pallas import tpu as pltpu
from jax.sharding import PartitionSpec as P


def extended(block, sides, width):
    for axis, dim in sides:
        count = lax.axis_size(axis)
        forward = [(i, i + 1) for i in range(count - 1)]
        forward.append((count - 1, 0))
        backward = [(target, source) for source, target in forward]
        low = lax.ppermute(
            lax.slice_in_dim(block, block.shape[dim] - width, None, axis=dim), axis, forward
        )
        high = lax.ppermute(lax.slice_in_dim(block, 0, width, axis=dim), axis, backward)
        block = jnp.concatenate([low, block, high], axis=dim)
    return block


def combined_all(value, axis, join):
    pieces = jax.tree.map(lambda part: lax.all_gather(part, axis), value)
    head = jax.tree.map(lambda part: part[0], pieces)
    tail = jax.tree.map(lambda part: part[1:], pieces)
    running, _ = lax.scan(lambda running, section: (join(running, section), None), head, tail)
    return running


def passed_along(value, axis, by):
    peers = lax.axis_size(axis)
    return lax.ppermute(value, axis, [(i, (i + by) % peers) for i in range(peers)])


def contract(form, left, right):
    if left.dtype == right.dtype:
        return jnp.einsum(
            form, left, right, preferred_element_type=jnp.float32, precision=lax.Precision.HIGHEST
        )
    return jnp.einsum(form, left.astype(jnp.float32), right, precision=lax.Precision.HIGHEST)


def inner(left, right):
    return lax.dot_general(
        left, right, (((0,), (0,)), ((), ())), preferred_element_type=jnp.float32
    )


def across(left, right):
    return lax.dot_general(
        left, right, (((1,), (1,)), ((), ())), preferred_element_type=jnp.float32
    )


def frame_pieces(frames):
    pieces = []
    offset = 0
    for degree in range(5):
        breadth = 2 * degree + 1
        square = frames[:, offset : offset + breadth * breadth].reshape(-1, breadth, breadth)
        offset = offset + breadth * breadth
        reach = min(degree, 2)
        pieces.append(square[:, degree - reach : degree + reach + 1, :])
    return pieces


def degree_slice(matrix, degree, channels):
    return matrix[:, degree * degree * channels : (degree + 1) * (degree + 1) * channels].reshape(
        matrix.shape[0], 2 * degree + 1, channels
    )


def group_coeffs(pieces):
    centre = [min(degree, 2) for degree in range(5)]
    order_zero = jnp.concatenate(
        [pieces[degree][:, centre[degree], :] for degree in range(5)], axis=1
    )
    order_one = jnp.concatenate(
        [pieces[degree][:, centre[degree] + 1, :] for degree in range(1, 5)]
        + [pieces[degree][:, centre[degree] - 1, :] for degree in range(1, 5)],
        axis=1,
    )
    order_two = jnp.concatenate(
        [pieces[degree][:, 4, :] for degree in range(2, 5)]
        + [pieces[degree][:, 0, :] for degree in range(2, 5)],
        axis=1,
    )
    return (order_zero, order_one, order_two)


def split_coeffs(order_zero, order_one, order_two, breadth):
    pieces = []
    for degree in range(5):
        stacked = [order_zero[:, degree * breadth : (degree + 1) * breadth]]
        if degree >= 1:
            stacked = (
                [order_one[:, (3 + degree) * breadth : (4 + degree) * breadth]]
                + stacked
                + [order_one[:, (degree - 1) * breadth : degree * breadth]]
            )
        if degree >= 2:
            stacked = (
                [order_two[:, (1 + degree) * breadth : (2 + degree) * breadth]]
                + stacked
                + [order_two[:, (degree - 2) * breadth : (degree - 1) * breadth]]
            )
        pieces.append(jnp.stack(stacked, axis=1))
    return pieces


def pair_matrix(weights):
    real_part = weights[0]
    imag_part = weights[1]
    return jnp.concatenate(
        [
            jnp.concatenate([real_part, imag_part], axis=1),
            jnp.concatenate([-imag_part, real_part], axis=1),
        ],
        axis=0,
    )


def spread_heads(weights, value_ch):
    return jnp.repeat(weights, value_ch // weights.shape[1], axis=1)


def spread_rows(factor, value_ch):
    return jnp.tile(spread_heads(factor, value_ch), (1, 25))


def edge_forward(source_rows, pieces, w_zero, w_one, w_two, alpha_w, edge_bias):
    channels = source_rows.shape[1] // 25
    value_ch = w_zero.shape[1] // 5
    rotated = [
        contract(
            "ekm,emc->ekc", pieces[degree], degree_slice(source_rows, degree, channels)
        ).astype(jnp.bfloat16)
        for degree in range(5)
    ]
    inputs = group_coeffs(rotated)
    out_zero = jnp.dot(inputs[0], w_zero, preferred_element_type=jnp.float32)
    out_one = jnp.dot(inputs[1], pair_matrix(w_one), preferred_element_type=jnp.float32)
    out_two = jnp.dot(inputs[2], pair_matrix(w_two), preferred_element_type=jnp.float32)
    scalar = out_zero[:, :value_ch]
    gate = jax.nn.silu(scalar).astype(jnp.bfloat16)
    logits = jnp.dot(gate, alpha_w, preferred_element_type=jnp.float32) + edge_bias
    values = split_coeffs(
        out_zero.astype(jnp.bfloat16),
        out_one.astype(jnp.bfloat16),
        out_two.astype(jnp.bfloat16),
        value_ch,
    )
    return (inputs, scalar, gate, logits, values)


def rotate_back(weights, values, pieces):
    value_ch = values[0].shape[2]
    spread = spread_heads(weights, value_ch)[:, None, :]
    outputs = [
        contract("ekm,ekv->emv", pieces[degree], values[degree].astype(jnp.float32) * spread)
        for degree in range(5)
    ]
    return jnp.concatenate([item.reshape(item.shape[0], -1) for item in outputs], axis=1)


def attention_grads(grad_back, values, pieces, heads):
    value_ch = values[0].shape[2]
    message_grads = [
        contract("ekm,emv->ekv", pieces[degree], degree_slice(grad_back, degree, value_ch))
        for degree in range(5)
    ]
    product = jnp.sum(message_grads[0] * values[0].astype(jnp.float32), axis=1)
    for degree in range(1, 5):
        product = product + jnp.sum(
            message_grads[degree] * values[degree].astype(jnp.float32), axis=1
        )
    head_grad = product.reshape(product.shape[0], heads, value_ch // heads).sum(axis=2)
    return (message_grads, head_grad)


def value_grads(message_grads, attention, logit_grad, scalar, alpha_w):
    value_ch = scalar.shape[1]
    spread = spread_heads(attention, value_ch)[:, None, :]
    grads = [item * spread for item in message_grads]
    order_zero, order_one, order_two = group_coeffs(grads)
    sigmoid = jax.nn.sigmoid(scalar)
    gate_grad = across(logit_grad, alpha_w) * sigmoid * (1.0 + scalar * (1.0 - sigmoid))
    order_zero = jnp.concatenate(
        [order_zero[:, :value_ch] + gate_grad, order_zero[:, value_ch:]], axis=1
    )
    return (
        order_zero.astype(jnp.bfloat16),
        order_one.astype(jnp.bfloat16),
        order_two.astype(jnp.bfloat16),
    )


def pair_grad(block, half_in, half_out):
    return jnp.stack(
        [
            block[:half_in, :half_out] + block[half_in:, half_out:],
            block[:half_in, half_out:] - block[half_in:, :half_out],
        ]
    )


def input_grads(inputs, grads, w_zero, w_one, w_two, pieces, channels):
    weight_zero = inner(inputs[0], grads[0])
    weight_one = pair_grad(inner(inputs[1], grads[1]), w_one.shape[1], w_one.shape[2])
    weight_two = pair_grad(inner(inputs[2], grads[2]), w_two.shape[1], w_two.shape[2])
    coeff_zero = across(grads[0], w_zero).astype(jnp.bfloat16)
    coeff_one = across(grads[1], pair_matrix(w_one)).astype(jnp.bfloat16)
    coeff_two = across(grads[2], pair_matrix(w_two)).astype(jnp.bfloat16)
    coeff_pieces = split_coeffs(coeff_zero, coeff_one, coeff_two, channels)
    row_grads = jnp.concatenate(
        [
            contract("ekm,ekc->emc", pieces[degree], coeff_pieces[degree]).reshape(
                coeff_zero.shape[0], -1
            )
            for degree in range(5)
        ],
        axis=1,
    )
    return ((weight_zero, weight_one, weight_two), row_grads)


def grouped_rows(item, groups):
    if item.ndim == 3:
        return jnp.transpose(
            item.reshape(2, groups, item.shape[1] // groups, item.shape[2]), (1, 0, 2, 3)
        ).reshape(groups, -1)
    return item.reshape(groups, -1)


def body(
    node_feats,
    frame_blocks,
    src_ids,
    dst_ids,
    edge_bias,
    w_zero,
    w_one,
    w_two,
    alpha_w,
    out_proj,
    grad_out,
):
    tile_rows = node_feats.shape[1]
    channels = node_feats.shape[2] // 25
    value_ch = w_zero.shape[1] // 5
    heads = alpha_w.shape[1]
    owners = lax.axis_size("graph")
    owner = lax.axis_index("graph")
    padded = extended(node_feats, (("graph", 1),), tile_rows)[0]
    sources = src_ids[0]
    targets = dst_ids[0] - owner * tile_rows
    slots = (sources // tile_rows - owner + 1 + owners) % owners * tile_rows + sources % tile_rows
    pieces = frame_pieces(frame_blocks[0])
    source_rows = jnp.take(padded, slots, axis=0)
    inputs, scalar, gate, logits, values = edge_forward(
        source_rows, pieces, w_zero, w_one, w_two, alpha_w, edge_bias[0]
    )
    local_max = jnp.maximum(
        jax.ops.segment_max(logits, targets, num_segments=tile_rows, indices_are_sorted=True), -1e30
    )
    raised = jnp.exp(logits - local_max[targets])
    local_total = jax.ops.segment_sum(
        raised, targets, num_segments=tile_rows, indices_are_sorted=True
    )
    local_acc = jax.ops.segment_sum(
        rotate_back(raised, values, pieces),
        targets,
        num_segments=tile_rows,
        indices_are_sorted=True,
    )

    def combine(earlier, later):
        highest = jnp.maximum(earlier[0], later[0])
        left_scale = jnp.exp(earlier[0] - highest)
        right_scale = jnp.exp(later[0] - highest)
        return (
            highest,
            earlier[1] * left_scale + later[1] * right_scale,
            earlier[2] * spread_rows(left_scale, value_ch)
            + later[2] * spread_rows(right_scale, value_ch),
        )

    highest, totals, summed = combined_all((local_max, local_total, local_acc), "sub", combine)
    summed_half = (summed / spread_rows(totals, value_ch)).astype(jnp.bfloat16)
    attention = jnp.exp(logits - highest[targets]) / totals[targets]
    own_rows = node_feats[0]
    projected = jnp.dot(
        summed_half.reshape(-1, value_ch), out_proj, preferred_element_type=jnp.float32
    ).reshape(tile_rows, -1)
    updated = (own_rows.astype(jnp.float32) + projected).astype(jnp.bfloat16)
    own_grad = grad_out[0]
    half_rows = tile_rows // lax.axis_size("sub")
    half_start = lax.axis_index("sub") * half_rows
    summed_share = lax.dynamic_slice_in_dim(summed_half, half_start, half_rows, 0)
    grad_share = lax.dynamic_slice_in_dim(own_grad, half_start, half_rows, 0)
    proj_grad = inner(summed_share.reshape(-1, value_ch), grad_share.reshape(-1, channels))
    summed_grad = across(own_grad.reshape(-1, channels), out_proj).reshape(tile_rows, -1)
    message_grads, head_grad = attention_grads(summed_grad[targets], values, pieces, heads)
    local_dots = jax.ops.segment_sum(
        attention * head_grad, targets, num_segments=tile_rows, indices_are_sorted=True
    )
    dots = lax.psum(local_dots, "sub")
    logit_grad = (attention * (head_grad - dots[targets])).astype(jnp.bfloat16)
    alpha_grad = inner(gate, logit_grad)
    grads = value_grads(message_grads, attention, logit_grad, scalar, alpha_w)
    conv_grads, row_grads = input_grads(inputs, grads, w_zero, w_one, w_two, pieces, channels)
    buffer_grads = jax.ops.segment_sum(row_grads, slots, num_segments=3 * tile_rows)
    from_after = passed_along(buffer_grads[:tile_rows].astype(jnp.bfloat16), "graph", -1).astype(
        jnp.float32
    )
    from_before = passed_along(
        buffer_grads[2 * tile_rows :].astype(jnp.bfloat16), "graph", 1
    ).astype(jnp.float32)
    own_total = buffer_grads[tile_rows : 2 * tile_rows] + from_after + from_before
    node_share = lax.psum_scatter(
        own_total.astype(jnp.bfloat16), "sub", scatter_dimension=0, tiled=True
    ).astype(jnp.float32)
    grad_nodes = node_share + grad_share.astype(jnp.float32)
    terms = conv_grads + (alpha_grad, proj_grad)
    groups = lax.axis_size("graph") * lax.axis_size("sub")
    flattened = jnp.concatenate([grouped_rows(item, groups) for item in terms], axis=1)
    share = lax.psum_scatter(
        flattened.astype(jnp.bfloat16), ("graph", "sub"), scatter_dimension=0, tiled=True
    ).astype(jnp.float32)
    share = lax.psum(share.astype(jnp.bfloat16), "dp").astype(jnp.float32)[0]
    results = []
    offset = 0
    for item in terms:
        count = item.size // groups
        piece = share[offset : offset + count]
        if item.ndim == 3:
            results.append(piece.reshape(2, item.shape[1] // groups, item.shape[2]))
        else:
            results.append(piece.reshape(item.shape[0] // groups, item.shape[1]))
        offset = offset + count
    return (
        updated[None],
        grad_nodes[None],
        results[0],
        results[1],
        results[2],
        results[3],
        results[4],
    )


def column(degree, order):
    if order == 0:
        return degree
    if order == 1:
        return 5 + degree - 1
    if order == -1:
        return 9 + degree - 1
    if order == 2:
        return 13 + degree - 2
    return 16 + degree - 2


def frame_entries():
    entries = []
    offset = 0
    for degree in range(5):
        breadth = 2 * degree + 1
        reach = min(degree, 2)
        for order in range(-reach, reach + 1):
            for full in range(breadth):
                entries.append((degree, order, full, offset + (degree + order) * breadth + full))
        offset += breadth * breadth
    return entries


ENTRIES = frame_entries()
INDEX = {(d, o, f): i for i, (d, o, f, _) in enumerate(ENTRIES)}
LANES = 128
STEP = 16
F32 = jnp.float32
BF16 = jnp.bfloat16


def exact(left, right):
    return jnp.dot(left, right, preferred_element_type=F32, precision=lax.Precision.HIGHEST)


def fast(left, right):
    return jnp.dot(left, right, preferred_element_type=F32)


def lanes(index, count=1):
    return slice(index * LANES, (index + count) * LANES)


def fused(
    graphs, dps, parts,
    nf, fr, src, dst, bias, w0_in, w1_in, w2_in, aw, op, go,
    upd, gn, tiles_out,
    w0, w1, w2,
    halo, small, small_in, acc_out, acc_in, fb, gp, sr, mg, zz, vv, weight, bk, gg, ig, rg, ng, ng_core, ng_sum, ng_in,
    wg, r1, hh, r2, kk, r3, fin,
    load_sem, halo_send, halo_recv, small_send, small_recv, acc_send, acc_recv, ng_send, ng_recv,
    s1s, s1r, s2s, s2r, s3s, s3r, s4s, s4r,
):
    edges = fr.shape[0]
    rows_dev = nf.shape[0]
    heads = aw.shape[0]
    g = lax.axis_index("graph")
    s = lax.axis_index("sub")
    d = lax.axis_index("dp")
    other = 1 - s

    def along(k):
        return lax.rem(g + k + graphs, graphs)

    def dp_along(k):
        return lax.rem(d + k, dps)

    def remote(source, target, send, recv, device):
        return pltpu.make_async_remote_copy(
            src_ref=source, dst_ref=target, send_sem=send, recv_sem=recv,
            device_id=device, device_id_type=pl.DeviceIdType.MESH,
        )

    loads = [
        pltpu.make_async_copy(source, target, load_sem.at[i])
        for i, (source, target) in enumerate(((w0_in, w0), (w1_in, w1), (w2_in, w2)))
    ]
    for load in loads:
        load.start()

    barrier = pltpu.get_barrier_semaphore()
    peers = [{"sub": other}]
    for k in range(1, graphs):
        peers.append({"graph": along(k)})
    for k in range(1, dps):
        peers.append({"dp": dp_along(k)})
    for peer in peers:
        pl.semaphore_signal(barrier, inc=1, device_id=peer, device_id_type=pl.DeviceIdType.MESH)
    pl.semaphore_wait(barrier, len(peers))

    section = nf.at[:, pl.ds(pl.multiple_of(s * 12 * LANES, LANES), 13 * LANES)]
    halos = [
        remote(section, halo.at[s, i], halo_send.at[i], halo_recv.at[i], {"graph": along(step)})
        for i, step in enumerate((1, -1))
    ]
    for copy in halos:
        copy.start()

    src_row = src[...]
    dst_row = dst[...]
    eye = lax.broadcasted_iota(jnp.int32, (edges, edges), 0) == lax.broadcasted_iota(
        jnp.int32, (edges, edges), 1
    )

    def to_column(row):
        spread = jnp.where(eye, jnp.broadcast_to(row.astype(F32), (edges, edges)), 0.0)
        return jnp.sum(spread, axis=1, keepdims=True).astype(jnp.int32)

    src_col = to_column(src_row)
    dst_col = to_column(dst_row) - g * rows_dev
    lane48 = lax.broadcasted_iota(jnp.int32, (edges, 3 * rows_dev), 1)
    row48 = lax.broadcasted_iota(jnp.int32, (3 * rows_dev, edges), 0)

    def block_ids(position):
        low = along(-1) * rows_dev + position
        mid = g * rows_dev + position - rows_dev
        high = along(1) * rows_dev + position - 2 * rows_dev
        return jnp.where(
            position < rows_dev, low, jnp.where(position < 2 * rows_dev, mid, high)
        )

    def hot(match, dtype=BF16):
        return jnp.where(match, 1.0, 0.0).astype(dtype)

    pick_src = hot(block_ids(lane48) == src_col)
    put_src = hot(block_ids(row48) == src_row)
    pick_dst = hot(lax.broadcasted_iota(jnp.int32, (edges, rows_dev), 1) == dst_col)
    put_dst = hot(
        lax.broadcasted_iota(jnp.int32, (rows_dev, edges), 0) == dst_row - g * rows_dev
    )
    lane_j = lax.broadcasted_iota(jnp.int32, (edges, LANES), 1)
    mine = lax.shift_right_logical(lane_j, 3) == dst_col
    sq0 = lax.broadcasted_iota(jnp.int32, (LANES, LANES), 0)
    sq1 = lax.broadcasted_iota(jnp.int32, (LANES, LANES), 1)
    spread = hot(jnp.bitwise_and(sq0, 7) == lax.shift_right_logical(sq1, 4), F32)
    gather_heads = hot(lax.shift_right_logical(sq0, 4) == jnp.bitwise_and(sq1, 7), F32)
    compact = hot(jnp.bitwise_and(sq0, 7) == sq1)
    tile_heads = hot(
        lax.broadcasted_iota(jnp.int32, (heads, LANES), 0)
        == jnp.bitwise_and(lax.broadcasted_iota(jnp.int32, (heads, LANES), 1), 7),
        F32,
    )
    alpha_t = inner(aw[...], tile_heads.astype(BF16)).astype(BF16)
    proj = op[...]

    for k in range(25):
        rows = fast(pick_dst, go[:, lanes(k)]).astype(BF16)
        gp[:, lanes(k)] = across(rows, proj)

    def message_step(c, _):
        at = pl.ds(pl.multiple_of(c * STEP, STEP), STEP)
        frames = fr[at, :].astype(F32)
        for degree in range(5):
            reach = min(degree, 2)
            breadth = 2 * degree + 1
            inputs = [gp[at, lanes(degree * degree + f)] for f in range(breadth)]
            for order in range(-reach, reach + 1):
                total = None
                for f in range(breadth):
                    i = INDEX[(degree, order, f)]
                    col = ENTRIES[i][3]
                    value = jnp.broadcast_to(frames[:, col : col + 1], (STEP, LANES))
                    fb[i, at, :] = value
                    term = value * inputs[f]
                    total = term if total is None else total + term
                mg[at, lanes(column(degree, order))] = total
        return 0

    lax.fori_loop(0, edges // STEP, message_step, 0)

    shared = [
        remote(halo.at[s, i], halo.at[s, i], halo_send.at[2 + i], halo_recv.at[2 + i], {"sub": other})
        for i in range(2)
    ]
    for i in range(2):
        halos[i].wait()
        shared[i].start()
    for copy in shared:
        copy.wait()
    for k in range(25):
        h = 0 if k < 13 else 1
        at = lanes(k - 12 * h)
        block = jnp.concatenate([halo[h, 0, :, at], nf[:, lanes(k)], halo[h, 1, :, at]], axis=0)
        sr[:, lanes(k)] = fast(pick_src, block)

    def rotate_step(c, _):
        at = pl.ds(pl.multiple_of(c * STEP, STEP), STEP)
        for degree in range(5):
            reach = min(degree, 2)
            breadth = 2 * degree + 1
            inputs = [sr[at, lanes(degree * degree + f)] for f in range(breadth)]
            for order in range(-reach, reach + 1):
                total = None
                for f in range(breadth):
                    term = fb[INDEX[(degree, order, f)], at, :] * inputs[f]
                    total = term if total is None else total + term
                zz[at, lanes(column(degree, order))] = total.astype(BF16)
        return 0

    lax.fori_loop(0, edges // STEP, rotate_step, 0)

    for load in loads:
        load.wait()
    z0 = zz[:, lanes(0, 5)]
    zp1, zm1 = zz[:, lanes(5, 4)], zz[:, lanes(9, 4)]
    zp2, zm2 = zz[:, lanes(13, 3)], zz[:, lanes(16, 3)]
    y0 = fast(z0, w0[...])
    scalar = y0[:, :LANES]
    vv[:, lanes(0, 5)] = y0.astype(BF16)
    vv[:, lanes(5, 4)] = (fast(zp1, w1[0]) - fast(zm1, w1[1])).astype(BF16)
    vv[:, lanes(9, 4)] = (fast(zp1, w1[1]) + fast(zm1, w1[0])).astype(BF16)
    vv[:, lanes(13, 3)] = (fast(zp2, w2[0]) - fast(zm2, w2[1])).astype(BF16)
    vv[:, lanes(16, 3)] = (fast(zp2, w2[1]) + fast(zm2, w2[0])).astype(BF16)
    bias_lanes = lax.dot_general(
        bias[...], tile_heads, (((0,), (0,)), ((), ())),
        preferred_element_type=F32, precision=lax.Precision.HIGHEST,
    )
    sigmoid = lax.logistic(scalar)
    gate = (scalar * sigmoid).astype(BF16)
    logits = fast(gate, alpha_t) + bias_lanes
    logits = jnp.where(mine, logits, -1e30)
    product = None
    for k in range(19):
        term = mg[:, lanes(k)] * vv[:, lanes(k)].astype(F32)
        product = term if product is None else product + term
    head_grad = exact(product, gather_heads)
    peak = jnp.max(logits, axis=0, keepdims=True)
    raised = jnp.where(mine, jnp.exp(logits - peak), 0.0)
    total = jnp.sum(raised, axis=0, keepdims=True)
    dots = jnp.sum(raised * head_grad, axis=0, keepdims=True)
    small[0:1, :] = peak
    small[1:2, :] = total
    small[2:3, :] = dots
    small[3:8, :] = jnp.zeros((5, LANES), F32)
    small_copy = remote(small, small_in, small_send, small_recv, {"sub": other})
    small_copy.start()

    weight[...] = exact(raised, spread)

    def back_step(c, _):
        at = pl.ds(pl.multiple_of(c * STEP, STEP), STEP)
        scale = weight[at, :]
        for degree in range(5):
            reach = min(degree, 2)
            orders = range(-reach, reach + 1)
            inputs = {o: vv[at, lanes(column(degree, o))].astype(F32) * scale for o in orders}
            for f in range(2 * degree + 1):
                out = None
                for o in orders:
                    term = fb[INDEX[(degree, o, f)], at, :] * inputs[o]
                    out = term if out is None else out + term
                bk[at, lanes(degree * degree + f)] = out.astype(BF16)
        return 0

    lax.fori_loop(0, edges // STEP, back_step, 0)
    small_copy.wait()
    peak_in = small_in[0:1, :]
    top = jnp.maximum(peak, peak_in)
    own_scale = jnp.exp(peak - top)
    in_scale = jnp.exp(peak_in - top)
    whole = total * own_scale + small_in[1:2, :] * in_scale
    all_dots = (dots * own_scale + small_in[2:3, :] * in_scale) / whole
    node_lane = lax.broadcasted_iota(jnp.int32, (rows_dev, LANES), 1)
    node_row = lax.broadcasted_iota(jnp.int32, (rows_dev, LANES), 0)
    node_scale = exact(
        jnp.where(lax.shift_right_logical(node_lane, 3) == node_row, own_scale / whole, 0.0), spread
    )
    for k in range(25):
        acc_out[:, lanes(k)] = fast(put_dst, bk[:, lanes(k)]) * node_scale
    acc_copy = remote(acc_out, acc_in, acc_send, acc_recv, {"sub": other})
    acc_copy.start()

    attention = raised * (own_scale / whole)
    logit_grad = (attention * (head_grad - all_dots)).astype(BF16)
    spread_att = exact(attention, spread)
    gate_grad = across(logit_grad, alpha_t) * sigmoid * (1.0 + scalar * (1.0 - sigmoid))
    for k in range(19):
        grad = mg[:, lanes(k)] * spread_att
        if k == 0:
            grad = grad + gate_grad
        gg[:, lanes(k)] = grad.astype(BF16)

    groups = graphs * 2

    def put(piece, base, rows_share, row0, matrix):
        wide = matrix.shape[1] // LANES
        part = wg[piece].shape[3]
        for i in range(matrix.shape[0] // STEP):
            row = row0 + i * STEP
            group = row // rows_share
            inner_row = (row % rows_share) // STEP
            for j in range(wide):
                tile = base + inner_row * wide + j
                wg[piece][group % 2, tile // part, group // 2, tile % part] = matrix[
                    i * STEP : (i + 1) * STEP, lanes(j)
                ].astype(BF16)

    def zero_tail(piece, used):
        part = wg[piece].shape[3]
        for tile in range(used, part * dps):
            wg[piece][:, tile // part, :, tile % part] = jnp.zeros((2, graphs, STEP, LANES), BF16)

    def stage_one(piece):
        return remote(
            wg[piece].at[other], r1[piece], s1s.at[piece], s1r.at[piece], {"sub": other}
        )

    def stage_two(piece):
        return [
            remote(
                hh[piece].at[dp_along(k)], r2[piece].at[k - 1],
                s2s.at[piece, k - 1], s2r.at[piece, k - 1], {"dp": dp_along(k)},
            )
            for k in range(1, dps)
        ]

    def stage_three(piece):
        return [
            remote(
                kk[piece].at[along(k)], r3[piece].at[k - 1],
                s3s.at[piece, k - 1], s3r.at[piece, k - 1], {"graph": along(k)},
            )
            for k in range(1, graphs)
        ]

    def stage_four(piece):
        return [
            remote(
                fin[piece].at[0], fin[piece].at[k],
                s4s.at[piece, k - 1], s4r.at[piece, k - 1], {"dp": dp_along(k)},
            )
            for k in range(1, dps)
        ]

    def start(copies):
        for copy in copies:
            copy.start()
        return copies

    def wait(copies):
        for copy in copies:
            copy.wait()

    gp1, gm1 = gg[:, lanes(5, 4)], gg[:, lanes(9, 4)]
    rows1 = 512 // groups
    one = [None] * 4
    tiles1 = (rows1 // STEP) * 4
    for b in range(4):
        put(0, 0, rows1, b * LANES, inner(zz[:, lanes(5 + b)], gp1) + inner(zz[:, lanes(9 + b)], gm1))
    zero_tail(0, tiles1)
    one[0] = stage_one(0)
    one[0].start()
    for b in range(4):
        put(1, 0, rows1, b * LANES, inner(zz[:, lanes(5 + b)], gm1) - inner(zz[:, lanes(9 + b)], gp1))
    zero_tail(1, tiles1)
    one[1] = stage_one(1)
    one[1].start()

    g0 = gg[:, lanes(0, 5)]
    rows0 = 640 // groups
    for b in range(5):
        put(2, 0, rows0, b * LANES, inner(zz[:, lanes(b)], g0))
    alpha_rows = LANES // groups
    tiles0 = (rows0 // STEP) * 5
    logit_small = fast(logit_grad, compact).astype(BF16)
    put(2, tiles0, alpha_rows, 0, inner(gate, logit_small))
    zero_tail(2, tiles0 + alpha_rows // STEP)
    one[2] = stage_one(2)
    one[2].start()

    def add_one(piece):
        one[piece].wait()
        for p in range(dps):
            hh[piece][p] = wg[piece][s, p] + r1[piece][p]
        return start(stage_two(piece))

    def add_two(piece):
        wait(two[piece])
        if dps == 2:
            kk[piece][...] = hh[piece][d] + r2[piece][0]
        else:
            value = hh[piece][d].astype(F32)
            for k in range(1, dps):
                value = value + r2[piece][k - 1].astype(F32)
            kk[piece][...] = value.astype(BF16)
        return start(stage_three(piece))

    def add_three(piece):
        wait(three[piece])
        value = kk[piece][g].astype(F32)
        for k in range(1, graphs):
            value = value + r3[piece][k - 1].astype(F32)
        fin[piece][0] = value.astype(BF16)
        return start(stage_four(piece))

    two = [None] * 4
    three = [None] * 4
    four = [None] * 4
    two[0] = add_one(0)

    acc_copy.wait()
    summed = jnp.concatenate(
        [(acc_out[:, lanes(k)] + acc_in[:, lanes(k)]).astype(BF16) for k in range(25)], axis=0
    )
    cotangent = jnp.concatenate([go[:, lanes(k)] for k in range(25)], axis=0)
    half = rows_dev // 2
    in_half = lax.broadcasted_iota(jnp.int32, summed.shape, 0)
    in_half = lax.shift_right_logical(jnp.bitwise_and(in_half, rows_dev - 1), 3) == s
    share = jnp.where(in_half, summed.astype(F32), 0.0).astype(BF16)
    gp2, gm2 = gg[:, lanes(13, 3)], gg[:, lanes(16, 3)]
    rows2 = 384 // groups
    tiles2 = (rows2 // STEP) * 3
    for b in range(3):
        zp, zm = zz[:, lanes(13 + b)], zz[:, lanes(16 + b)]
        put(3, 0, rows2, b * LANES, inner(zp, gp2) + inner(zm, gm2))
        put(3, tiles2, rows2, b * LANES, inner(zp, gm2) - inner(zm, gp2))
    put(3, 2 * tiles2, alpha_rows, 0, inner(share, cotangent))
    zero_tail(3, 2 * tiles2 + alpha_rows // STEP)
    one[3] = stage_one(3)
    one[3].start()
    two[1] = add_one(1)

    ig[:, lanes(0, 5)] = across(g0, w0[...]).astype(BF16)
    ig[:, lanes(5, 4)] = (across(gp1, w1[0]) + across(gm1, w1[1])).astype(BF16)
    two[2] = add_one(2)
    ig[:, lanes(9, 4)] = (across(gm1, w1[0]) - across(gp1, w1[1])).astype(BF16)
    ig[:, lanes(13, 3)] = (across(gp2, w2[0]) + across(gm2, w2[1])).astype(BF16)
    ig[:, lanes(16, 3)] = (across(gm2, w2[0]) - across(gp2, w2[1])).astype(BF16)
    two[3] = add_one(3)

    def row_step(c, _):
        at = pl.ds(pl.multiple_of(c * STEP, STEP), STEP)
        for degree in range(5):
            reach = min(degree, 2)
            orders = range(-reach, reach + 1)
            inputs = {o: ig[at, lanes(column(degree, o))].astype(F32) for o in orders}
            for f in range(2 * degree + 1):
                out = None
                for o in orders:
                    term = fb[INDEX[(degree, o, f)], at, :] * inputs[o]
                    out = term if out is None else out + term
                rg[at, lanes(degree * degree + f)] = out.astype(BF16)
        return 0

    lax.fori_loop(0, edges // STEP, row_step, 0)

    three[0] = add_two(0)
    for k in range(13):
        low = fast(put_src, rg[:, lanes(k)])
        high = fast(put_src, rg[:, lanes(13 + k)]) if k < 12 else jnp.zeros_like(low)
        for b in range(3):
            for h in range(2):
                at = slice(b * rows_dev + h * half, b * rows_dev + (h + 1) * half)
                ng[h, b, :, lanes(k)] = jnp.concatenate([low[at], high[at]], axis=0).astype(BF16)
    node_core = remote(ng.at[other], ng_core, ng_send.at[0], ng_recv.at[0], {"sub": other})
    node_core.start()
    three[1] = add_two(1)
    node_core.wait()
    ng_sum[...] = ng[s] + ng_core[...]
    node_copies = [
        remote(ng_sum.at[2 * i], ng_in.at[i], ng_send.at[1 + i], ng_recv.at[1 + i], {"graph": along(step)})
        for i, step in enumerate((-1, 1))
    ]
    start(node_copies)

    projected = fast(summed, proj)
    for k in range(25):
        upd[:, lanes(k)] = (
            nf[:, lanes(k)].astype(F32) + projected[k * rows_dev : (k + 1) * rows_dev]
        ).astype(BF16)
    three[2] = add_two(2)

    three[3] = add_two(3)
    wait(node_copies)
    for k in range(13):
        value = ng[s, 1, :, lanes(k)].astype(F32) + ng_core[1, :, lanes(k)].astype(F32)
        value = value + ng_in[0, :, lanes(k)].astype(F32) + ng_in[1, :, lanes(k)].astype(F32)
        for part, coef in ((0, k), (1, 13 + k)):
            if coef < 25:
                base = go[:, lanes(coef)].astype(F32)
                base = jnp.where(s == 0, base[:half], base[half:])
                gn[:, lanes(coef)] = value[part * half : (part + 1) * half] + base

    for piece in range(4):
        four[piece] = add_three(piece)
    base = 0
    for piece, count in enumerate(
        (tiles1, tiles1, tiles0 + alpha_rows // STEP, 2 * tiles2 + alpha_rows // STEP)
    ):
        wait(four[piece])
        part = fin[piece].shape[1]
        for p in range(dps):
            size = min(part, count - p * part)
            if size > 0:
                at = base + p * part
                tiles_out[at : at + size] = fin[piece][lax.rem(d - p + dps, dps), :size]
        base += count


def unpack(upd, gn, tiles, upd_out, gn_out, o0, o1, o2, oa, oproj):
    upd_out[...] = upd[...]
    gn_out[...] = gn[...]
    base = 0

    def matrix(write, rows, wide):
        nonlocal base
        for i in range(rows // STEP):
            for j in range(wide):
                write(slice(i * STEP, (i + 1) * STEP), lanes(j), tiles[base].astype(F32))
                base += 1

    def into(ref, lead=None):
        def write(rows, columns, value):
            if lead is None:
                ref[rows, columns] = value
            else:
                ref[lead, rows, columns] = value

        return write

    for q in range(2):
        matrix(into(o1, q), o1.shape[1], 4)
    matrix(into(o0), o0.shape[0], 5)
    for i in range(oa.shape[1] // STEP):
        pick = lax.broadcasted_iota(jnp.int32, (oa.shape[0], LANES), 0) == lax.broadcasted_iota(
            jnp.int32, (oa.shape[0], LANES), 1
        )
        oa[:, i * STEP : (i + 1) * STEP] = across(
            jnp.where(pick, 1.0, 0.0).astype(BF16), tiles[base]
        )
        base += 1
    for q in range(2):
        matrix(into(o2, q), o2.shape[1], 3)
    matrix(into(oproj), oproj.shape[0], 1)


def fused_body(graphs, dps, parts):
    groups = graphs * 2

    def run(node_feats, frame_blocks, src_ids, dst_ids, edge_bias, w_zero, w_one, w_two, alpha_w, out_proj, grad_out):
        rows_dev = node_feats.shape[1]
        edges = frame_blocks.shape[1]
        heads = alpha_w.shape[1]
        used = (
            (512 // groups // STEP) * 4,
            (512 // groups // STEP) * 4,
            (640 // groups // STEP) * 5 + LANES // groups // STEP,
            2 * (384 // groups // STEP) * 3 + LANES // groups // STEP,
        )
        part = [-(-count // dps) for count in used]
        dma = pltpu.SemaphoreType.DMA
        wide = 25 * LANES
        kept = 19 * LANES

        def per_piece(lead):
            return [pltpu.VMEM((*lead(p), STEP, LANES), BF16) for p in part]

        scratch = [
            pltpu.VMEM(w_zero.shape, BF16),
            pltpu.VMEM(w_one.shape, BF16),
            pltpu.VMEM(w_two.shape, BF16),
            pltpu.VMEM((2, 2, rows_dev, 13 * LANES), BF16),
            pltpu.VMEM((8, LANES), F32),
            pltpu.VMEM((8, LANES), F32),
            pltpu.VMEM((rows_dev, wide), F32),
            pltpu.VMEM((rows_dev, wide), F32),
            pltpu.VMEM((len(ENTRIES), edges, LANES), F32),
            pltpu.VMEM((edges, wide), F32),
            pltpu.VMEM((edges, wide), F32),
            pltpu.VMEM((edges, kept), F32),
            pltpu.VMEM((edges, kept), BF16),
            pltpu.VMEM((edges, kept), BF16),
            pltpu.VMEM((edges, LANES), F32),
            pltpu.VMEM((edges, wide), BF16),
            pltpu.VMEM((edges, kept), BF16),
            pltpu.VMEM((edges, kept), BF16),
            pltpu.VMEM((edges, wide), BF16),
            pltpu.VMEM((2, 3, STEP, 13 * LANES), BF16),
            pltpu.VMEM((3, STEP, 13 * LANES), BF16),
            pltpu.VMEM((3, STEP, 13 * LANES), BF16),
            pltpu.VMEM((2, STEP, 13 * LANES), BF16),
            per_piece(lambda p: (2, dps, graphs, p)),
            per_piece(lambda p: (dps, graphs, p)),
            per_piece(lambda p: (dps, graphs, p)),
            per_piece(lambda p: (max(dps - 1, 1), graphs, p)),
            per_piece(lambda p: (graphs, p)),
            per_piece(lambda p: (graphs - 1, p)),
            per_piece(lambda p: (dps, p)),
            dma((3,)), dma((4,)), dma((4,)), dma, dma, dma, dma, dma((3,)), dma((3,)),
            dma((4,)), dma((4,)),
            dma((4, max(dps - 1, 1))), dma((4, max(dps - 1, 1))),
            dma((4, graphs - 1)), dma((4, graphs - 1)),
            dma((4, max(dps - 1, 1))), dma((4, max(dps - 1, 1))),
        ]
        flat = []
        counts = []
        for item in scratch:
            if isinstance(item, list):
                counts.append(len(item))
                flat.extend(item)
            else:
                counts.append(0)
                flat.append(item)

        def entry(*refs):
            lead, rest = refs[:14], list(refs[14:])
            grouped = []
            for count in counts:
                if count:
                    grouped.append(rest[:count])
                    rest = rest[count:]
                else:
                    grouped.append(rest.pop(0))
            fused(graphs, dps, parts, *lead, *grouped)

        vmem = pl.BlockSpec(memory_space=pltpu.VMEM)
        anywhere = pl.BlockSpec(memory_space=pl.ANY)
        count = sum(used)
        packed = pl.pallas_call(
            entry,
            out_shape=(
                jax.ShapeDtypeStruct((rows_dev, wide), BF16),
                jax.ShapeDtypeStruct((rows_dev // 2, wide), F32),
                jax.ShapeDtypeStruct((count, STEP, LANES), BF16),
            ),
            in_specs=[vmem] * 5 + [anywhere] * 3 + [vmem] * 3,
            out_specs=[vmem] * 3,
            scratch_shapes=flat,
            compiler_params=pltpu.CompilerParams(
                collective_id=0, has_side_effects=True, vmem_limit_bytes=56 * 1024 * 1024
            ),
        )(
            node_feats[0], frame_blocks[0], src_ids, dst_ids, edge_bias[0].T,
            w_zero, w_one, w_two, alpha_w.T, out_proj, grad_out[0],
        )
        out = pl.pallas_call(
            unpack,
            out_shape=(
                jax.ShapeDtypeStruct((rows_dev, wide), BF16),
                jax.ShapeDtypeStruct((rows_dev // 2, wide), F32),
                jax.ShapeDtypeStruct((640 // groups, 640), F32),
                jax.ShapeDtypeStruct((2, 512 // groups, 512), F32),
                jax.ShapeDtypeStruct((2, 384 // groups, 384), F32),
                jax.ShapeDtypeStruct((heads, LANES // groups), F32),
                jax.ShapeDtypeStruct((LANES // groups, LANES), F32),
            ),
            in_specs=[vmem] * 3,
            out_specs=[vmem] * 7,
        )(*packed)
        return (out[0][None], out[1][None], out[2], out[3], out[4], out[5].T, out[6])

    return run


def solution(mesh):
    placed = (
        P(("parts", "dp"), "graph", None),
        P(("parts", "dp"), ("graph", "sub"), None),
        P(("parts", "dp"), ("graph", "sub")),
        P(("parts", "dp"), ("graph", "sub")),
        P(("parts", "dp"), ("graph", "sub"), None),
        P(),
        P(),
        P(),
        P(),
        P(),
        P(("parts", "dp"), "graph", None),
    )
    graphs, dps = mesh.shape["graph"], mesh.shape["dp"]
    aligned = (128 // (graphs * 2)) % STEP == 0 and graphs >= 4 and mesh.shape["sub"] == 2
    return jax.shard_map(
        fused_body(graphs, dps, mesh.shape["parts"]) if aligned else body,
        mesh=mesh,
        in_specs=placed,
        out_specs=(
            P(("parts", "dp"), "graph", None),
            P(("parts", "dp"), ("graph", "sub"), None),
            P(("parts", "graph", "sub"), None),
            P("parts", ("graph", "sub"), None),
            P("parts", ("graph", "sub"), None),
            P(("parts", "graph", "sub"), None),
            P(("parts", "graph", "sub"), None),
        ),
        check_vma=False,
    )
```

```python
import jax
import jax.numpy as jnp
from jax import lax
from jax.experimental import pallas as pl
from jax.experimental.pallas import tpu as pltpu
from jax.sharding import PartitionSpec as P


def extended(block, sides, width):
    for axis, dim in sides:
        count = lax.axis_size(axis)
        forward = [(i, i + 1) for i in range(count - 1)]
        forward.append((count - 1, 0))
        backward = [(target, source) for source, target in forward]
        low = lax.ppermute(
            lax.slice_in_dim(block, block.shape[dim] - width, None, axis=dim), axis, forward
        )
        high = lax.ppermute(lax.slice_in_dim(block, 0, width, axis=dim), axis, backward)
        block = jnp.concatenate([low, block, high], axis=dim)
    return block


def combined_all(value, axis, join):
    pieces = jax.tree.map(lambda part: lax.all_gather(part, axis), value)
    head = jax.tree.map(lambda part: part[0], pieces)
    tail = jax.tree.map(lambda part: part[1:], pieces)
    running, _ = lax.scan(lambda running, section: (join(running, section), None), head, tail)
    return running


def passed_along(value, axis, by):
    peers = lax.axis_size(axis)
    return lax.ppermute(value, axis, [(i, (i + by) % peers) for i in range(peers)])


def contract(form, left, right):
    if left.dtype == right.dtype:
        return jnp.einsum(
            form, left, right, preferred_element_type=jnp.float32, precision=lax.Precision.HIGHEST
        )
    return jnp.einsum(form, left.astype(jnp.float32), right, precision=lax.Precision.HIGHEST)


def inner(left, right):
    return lax.dot_general(
        left, right, (((0,), (0,)), ((), ())), preferred_element_type=jnp.float32
    )


def across(left, right):
    return lax.dot_general(
        left, right, (((1,), (1,)), ((), ())), preferred_element_type=jnp.float32
    )


def frame_pieces(frames):
    pieces = []
    offset = 0
    for degree in range(5):
        breadth = 2 * degree + 1
        square = frames[:, offset : offset + breadth * breadth].reshape(-1, breadth, breadth)
        offset = offset + breadth * breadth
        reach = min(degree, 2)
        pieces.append(square[:, degree - reach : degree + reach + 1, :])
    return pieces


def degree_slice(matrix, degree, channels):
    return matrix[:, degree * degree * channels : (degree + 1) * (degree + 1) * channels].reshape(
        matrix.shape[0], 2 * degree + 1, channels
    )


def group_coeffs(pieces):
    centre = [min(degree, 2) for degree in range(5)]
    order_zero = jnp.concatenate(
        [pieces[degree][:, centre[degree], :] for degree in range(5)], axis=1
    )
    order_one = jnp.concatenate(
        [pieces[degree][:, centre[degree] + 1, :] for degree in range(1, 5)]
        + [pieces[degree][:, centre[degree] - 1, :] for degree in range(1, 5)],
        axis=1,
    )
    order_two = jnp.concatenate(
        [pieces[degree][:, 4, :] for degree in range(2, 5)]
        + [pieces[degree][:, 0, :] for degree in range(2, 5)],
        axis=1,
    )
    return (order_zero, order_one, order_two)


def split_coeffs(order_zero, order_one, order_two, breadth):
    pieces = []
    for degree in range(5):
        stacked = [order_zero[:, degree * breadth : (degree + 1) * breadth]]
        if degree >= 1:
            stacked = (
                [order_one[:, (3 + degree) * breadth : (4 + degree) * breadth]]
                + stacked
                + [order_one[:, (degree - 1) * breadth : degree * breadth]]
            )
        if degree >= 2:
            stacked = (
                [order_two[:, (1 + degree) * breadth : (2 + degree) * breadth]]
                + stacked
                + [order_two[:, (degree - 2) * breadth : (degree - 1) * breadth]]
            )
        pieces.append(jnp.stack(stacked, axis=1))
    return pieces


def pair_matrix(weights):
    real_part = weights[0]
    imag_part = weights[1]
    return jnp.concatenate(
        [
            jnp.concatenate([real_part, imag_part], axis=1),
            jnp.concatenate([-imag_part, real_part], axis=1),
        ],
        axis=0,
    )


def spread_heads(weights, value_ch):
    return jnp.repeat(weights, value_ch // weights.shape[1], axis=1)


def spread_rows(factor, value_ch):
    return jnp.tile(spread_heads(factor, value_ch), (1, 25))


def edge_forward(source_rows, pieces, w_zero, w_one, w_two, alpha_w, edge_bias):
    channels = source_rows.shape[1] // 25
    value_ch = w_zero.shape[1] // 5
    rotated = [
        contract(
            "ekm,emc->ekc", pieces[degree], degree_slice(source_rows, degree, channels)
        ).astype(jnp.bfloat16)
        for degree in range(5)
    ]
    inputs = group_coeffs(rotated)
    out_zero = jnp.dot(inputs[0], w_zero, preferred_element_type=jnp.float32)
    out_one = jnp.dot(inputs[1], pair_matrix(w_one), preferred_element_type=jnp.float32)
    out_two = jnp.dot(inputs[2], pair_matrix(w_two), preferred_element_type=jnp.float32)
    scalar = out_zero[:, :value_ch]
    gate = jax.nn.silu(scalar).astype(jnp.bfloat16)
    logits = jnp.dot(gate, alpha_w, preferred_element_type=jnp.float32) + edge_bias
    values = split_coeffs(
        out_zero.astype(jnp.bfloat16),
        out_one.astype(jnp.bfloat16),
        out_two.astype(jnp.bfloat16),
        value_ch,
    )
    return (inputs, scalar, gate, logits, values)


def rotate_back(weights, values, pieces):
    value_ch = values[0].shape[2]
    spread = spread_heads(weights, value_ch)[:, None, :]
    outputs = [
        contract("ekm,ekv->emv", pieces[degree], values[degree].astype(jnp.float32) * spread)
        for degree in range(5)
    ]
    return jnp.concatenate([item.reshape(item.shape[0], -1) for item in outputs], axis=1)


def attention_grads(grad_back, values, pieces, heads):
    value_ch = values[0].shape[2]
    message_grads = [
        contract("ekm,emv->ekv", pieces[degree], degree_slice(grad_back, degree, value_ch))
        for degree in range(5)
    ]
    product = jnp.sum(message_grads[0] * values[0].astype(jnp.float32), axis=1)
    for degree in range(1, 5):
        product = product + jnp.sum(
            message_grads[degree] * values[degree].astype(jnp.float32), axis=1
        )
    head_grad = product.reshape(product.shape[0], heads, value_ch // heads).sum(axis=2)
    return (message_grads, head_grad)


def value_grads(message_grads, attention, logit_grad, scalar, alpha_w):
    value_ch = scalar.shape[1]
    spread = spread_heads(attention, value_ch)[:, None, :]
    grads = [item * spread for item in message_grads]
    order_zero, order_one, order_two = group_coeffs(grads)
    sigmoid = jax.nn.sigmoid(scalar)
    gate_grad = across(logit_grad, alpha_w) * sigmoid * (1.0 + scalar * (1.0 - sigmoid))
    order_zero = jnp.concatenate(
        [order_zero[:, :value_ch] + gate_grad, order_zero[:, value_ch:]], axis=1
    )
    return (
        order_zero.astype(jnp.bfloat16),
        order_one.astype(jnp.bfloat16),
        order_two.astype(jnp.bfloat16),
    )


def pair_grad(block, half_in, half_out):
    return jnp.stack(
        [
            block[:half_in, :half_out] + block[half_in:, half_out:],
            block[:half_in, half_out:] - block[half_in:, :half_out],
        ]
    )


def input_grads(inputs, grads, w_zero, w_one, w_two, pieces, channels):
    weight_zero = inner(inputs[0], grads[0])
    weight_one = pair_grad(inner(inputs[1], grads[1]), w_one.shape[1], w_one.shape[2])
    weight_two = pair_grad(inner(inputs[2], grads[2]), w_two.shape[1], w_two.shape[2])
    coeff_zero = across(grads[0], w_zero).astype(jnp.bfloat16)
    coeff_one = across(grads[1], pair_matrix(w_one)).astype(jnp.bfloat16)
    coeff_two = across(grads[2], pair_matrix(w_two)).astype(jnp.bfloat16)
    coeff_pieces = split_coeffs(coeff_zero, coeff_one, coeff_two, channels)
    row_grads = jnp.concatenate(
        [
            contract("ekm,ekc->emc", pieces[degree], coeff_pieces[degree]).reshape(
                coeff_zero.shape[0], -1
            )
            for degree in range(5)
        ],
        axis=1,
    )
    return ((weight_zero, weight_one, weight_two), row_grads)


def grouped_rows(item, groups):
    if item.ndim == 3:
        return jnp.transpose(
            item.reshape(2, groups, item.shape[1] // groups, item.shape[2]), (1, 0, 2, 3)
        ).reshape(groups, -1)
    return item.reshape(groups, -1)


def body(
    node_feats,
    frame_blocks,
    src_ids,
    dst_ids,
    edge_bias,
    w_zero,
    w_one,
    w_two,
    alpha_w,
    out_proj,
    grad_out,
):
    tile_rows = node_feats.shape[1]
    channels = node_feats.shape[2] // 25
    value_ch = w_zero.shape[1] // 5
    heads = alpha_w.shape[1]
    owners = lax.axis_size("graph")
    owner = lax.axis_index("graph")
    padded = extended(node_feats, (("graph", 1),), tile_rows)[0]
    sources = src_ids[0]
    targets = dst_ids[0] - owner * tile_rows
    slots = (sources // tile_rows - owner + 1 + owners) % owners * tile_rows + sources % tile_rows
    pieces = frame_pieces(frame_blocks[0])
    source_rows = jnp.take(padded, slots, axis=0)
    inputs, scalar, gate, logits, values = edge_forward(
        source_rows, pieces, w_zero, w_one, w_two, alpha_w, edge_bias[0]
    )
    local_max = jnp.maximum(
        jax.ops.segment_max(logits, targets, num_segments=tile_rows, indices_are_sorted=True), -1e30
    )
    raised = jnp.exp(logits - local_max[targets])
    local_total = jax.ops.segment_sum(
        raised, targets, num_segments=tile_rows, indices_are_sorted=True
    )
    local_acc = jax.ops.segment_sum(
        rotate_back(raised, values, pieces),
        targets,
        num_segments=tile_rows,
        indices_are_sorted=True,
    )

    def combine(earlier, later):
        highest = jnp.maximum(earlier[0], later[0])
        left_scale = jnp.exp(earlier[0] - highest)
        right_scale = jnp.exp(later[0] - highest)
        return (
            highest,
            earlier[1] * left_scale + later[1] * right_scale,
            earlier[2] * spread_rows(left_scale, value_ch)
            + later[2] * spread_rows(right_scale, value_ch),
        )

    highest, totals, summed = combined_all((local_max, local_total, local_acc), "sub", combine)
    summed_half = (summed / spread_rows(totals, value_ch)).astype(jnp.bfloat16)
    attention = jnp.exp(logits - highest[targets]) / totals[targets]
    own_rows = node_feats[0]
    projected = jnp.dot(
        summed_half.reshape(-1, value_ch), out_proj, preferred_element_type=jnp.float32
    ).reshape(tile_rows, -1)
    updated = (own_rows.astype(jnp.float32) + projected).astype(jnp.bfloat16)
    own_grad = grad_out[0]
    half_rows = tile_rows // lax.axis_size("sub")
    half_start = lax.axis_index("sub") * half_rows
    summed_share = lax.dynamic_slice_in_dim(summed_half, half_start, half_rows, 0)
    grad_share = lax.dynamic_slice_in_dim(own_grad, half_start, half_rows, 0)
    proj_grad = inner(summed_share.reshape(-1, value_ch), grad_share.reshape(-1, channels))
    summed_grad = across(own_grad.reshape(-1, channels), out_proj).reshape(tile_rows, -1)
    message_grads, head_grad = attention_grads(summed_grad[targets], values, pieces, heads)
    local_dots = jax.ops.segment_sum(
        attention * head_grad, targets, num_segments=tile_rows, indices_are_sorted=True
    )
    dots = lax.psum(local_dots, "sub")
    logit_grad = (attention * (head_grad - dots[targets])).astype(jnp.bfloat16)
    alpha_grad = inner(gate, logit_grad)
    grads = value_grads(message_grads, attention, logit_grad, scalar, alpha_w)
    conv_grads, row_grads = input_grads(inputs, grads, w_zero, w_one, w_two, pieces, channels)
    buffer_grads = jax.ops.segment_sum(row_grads, slots, num_segments=3 * tile_rows)
    from_after = passed_along(buffer_grads[:tile_rows].astype(jnp.bfloat16), "graph", -1).astype(
        jnp.float32
    )
    from_before = passed_along(
        buffer_grads[2 * tile_rows :].astype(jnp.bfloat16), "graph", 1
    ).astype(jnp.float32)
    own_total = buffer_grads[tile_rows : 2 * tile_rows] + from_after + from_before
    node_share = lax.psum_scatter(
        own_total.astype(jnp.bfloat16), "sub", scatter_dimension=0, tiled=True
    ).astype(jnp.float32)
    grad_nodes = node_share + grad_share.astype(jnp.float32)
    terms = conv_grads + (alpha_grad, proj_grad)
    groups = lax.axis_size("graph") * lax.axis_size("sub")
    flattened = jnp.concatenate([grouped_rows(item, groups) for item in terms], axis=1)
    share = lax.psum_scatter(
        flattened.astype(jnp.bfloat16), ("graph", "sub"), scatter_dimension=0, tiled=True
    ).astype(jnp.float32)
    share = lax.psum(share.astype(jnp.bfloat16), "dp").astype(jnp.float32)[0]
    results = []
    offset = 0
    for item in terms:
        count = item.size // groups
        piece = share[offset : offset + count]
        if item.ndim == 3:
            results.append(piece.reshape(2, item.shape[1] // groups, item.shape[2]))
        else:
            results.append(piece.reshape(item.shape[0] // groups, item.shape[1]))
        offset = offset + count
    return (
        updated[None],
        grad_nodes[None],
        results[0],
        results[1],
        results[2],
        results[3],
        results[4],
    )


def column(degree, order):
    if order == 0:
        return degree
    if order == 1:
        return 5 + degree - 1
    if order == -1:
        return 9 + degree - 1
    if order == 2:
        return 13 + degree - 2
    return 16 + degree - 2


def frame_entries():
    entries = []
    offset = 0
    for degree in range(5):
        breadth = 2 * degree + 1
        reach = min(degree, 2)
        for order in range(-reach, reach + 1):
            for full in range(breadth):
                entries.append((degree, order, full, offset + (degree + order) * breadth + full))
        offset += breadth * breadth
    return entries


ENTRIES = frame_entries()
INDEX = {(d, o, f): i for i, (d, o, f, _) in enumerate(ENTRIES)}
LANES = 128
STEP = 16
F32 = jnp.float32
BF16 = jnp.bfloat16


def exact(left, right):
    return jnp.dot(left, right, preferred_element_type=F32, precision=lax.Precision.HIGHEST)


def fast(left, right):
    return jnp.dot(left, right, preferred_element_type=F32)


def lanes(index, count=1):
    return slice(index * LANES, (index + count) * LANES)


def fused(
    graphs, dps, parts,
    nf, fr, src, dst, bias, w0_in, w1_in, w2_in, aw, op, go,
    upd, gn, tiles_out,
    w0, w1, w2,
    halo, small, small_in, acc_out, acc_in, fb, gp, sr, mg, zz, vv, weight, bk, gg, ig, rg, ng, ng_core, ng_sum, ng_in,
    wg, r1, hh, r2, kk, r3, fin,
    load_sem, halo_send, halo_recv, small_send, small_recv, acc_send, acc_recv, ng_send, ng_recv,
    s1s, s1r, s2s, s2r, s3s, s3r, s4s, s4r,
):
    edges = fr.shape[0]
    rows_dev = nf.shape[0]
    heads = aw.shape[0]
    g = lax.axis_index("graph")
    s = lax.axis_index("sub")
    d = lax.axis_index("dp")
    other = 1 - s

    def along(k):
        return lax.rem(g + k + graphs, graphs)

    def dp_along(k):
        return lax.rem(d + k, dps)

    def remote(source, target, send, recv, device):
        return pltpu.make_async_remote_copy(
            src_ref=source, dst_ref=target, send_sem=send, recv_sem=recv,
            device_id=device, device_id_type=pl.DeviceIdType.MESH,
        )

    loads = [
        pltpu.make_async_copy(source, target, load_sem.at[i])
        for i, (source, target) in enumerate(((w0_in, w0), (w1_in, w1), (w2_in, w2)))
    ]
    for load in loads:
        load.start()

    barrier = pltpu.get_barrier_semaphore()
    peers = [{"sub": other}]
    for k in range(1, graphs):
        peers.append({"graph": along(k)})
    for k in range(1, dps):
        peers.append({"dp": dp_along(k)})
    for peer in peers:
        pl.semaphore_signal(barrier, inc=1, device_id=peer, device_id_type=pl.DeviceIdType.MESH)
    pl.semaphore_wait(barrier, len(peers))

    section = nf.at[:, pl.ds(pl.multiple_of(s * 12 * LANES, LANES), 13 * LANES)]
    halos = [
        remote(section, halo.at[s, i], halo_send.at[i], halo_recv.at[i], {"graph": along(step)})
        for i, step in enumerate((1, -1))
    ]
    for copy in halos:
        copy.start()

    src_row = src[...]
    dst_row = dst[...]
    eye = lax.broadcasted_iota(jnp.int32, (edges, edges), 0) == lax.broadcasted_iota(
        jnp.int32, (edges, edges), 1
    )

    def to_column(row):
        spread = jnp.where(eye, jnp.broadcast_to(row.astype(F32), (edges, edges)), 0.0)
        return jnp.sum(spread, axis=1, keepdims=True).astype(jnp.int32)

    src_col = to_column(src_row)
    dst_col = to_column(dst_row) - g * rows_dev
    lane48 = lax.broadcasted_iota(jnp.int32, (edges, 3 * rows_dev), 1)
    row48 = lax.broadcasted_iota(jnp.int32, (3 * rows_dev, edges), 0)

    def block_ids(position):
        low = along(-1) * rows_dev + position
        mid = g * rows_dev + position - rows_dev
        high = along(1) * rows_dev + position - 2 * rows_dev
        return jnp.where(
            position < rows_dev, low, jnp.where(position < 2 * rows_dev, mid, high)
        )

    def hot(match, dtype=BF16):
        return jnp.where(match, 1.0, 0.0).astype(dtype)

    pick_src = hot(block_ids(lane48) == src_col)
    put_src = hot(block_ids(row48) == src_row)
    pick_dst = hot(lax.broadcasted_iota(jnp.int32, (edges, rows_dev), 1) == dst_col)
    put_dst = hot(
        lax.broadcasted_iota(jnp.int32, (rows_dev, edges), 0) == dst_row - g * rows_dev
    )
    lane_j = lax.broadcasted_iota(jnp.int32, (edges, LANES), 1)
    mine = lax.shift_right_logical(lane_j, 3) == dst_col
    sq0 = lax.broadcasted_iota(jnp.int32, (LANES, LANES), 0)
    sq1 = lax.broadcasted_iota(jnp.int32, (LANES, LANES), 1)
    spread = hot(jnp.bitwise_and(sq0, 7) == lax.shift_right_logical(sq1, 4), F32)
    gather_heads = hot(lax.shift_right_logical(sq0, 4) == jnp.bitwise_and(sq1, 7), F32)
    compact = hot(jnp.bitwise_and(sq0, 7) == sq1)
    tile_heads = hot(
        lax.broadcasted_iota(jnp.int32, (heads, LANES), 0)
        == jnp.bitwise_and(lax.broadcasted_iota(jnp.int32, (heads, LANES), 1), 7),
        F32,
    )
    alpha_t = inner(aw[...], tile_heads.astype(BF16)).astype(BF16)
    proj = op[...]

    for k in range(25):
        rows = fast(pick_dst, go[:, lanes(k)]).astype(BF16)
        gp[:, lanes(k)] = across(rows, proj)

    def message_step(c, _):
        at = pl.ds(pl.multiple_of(c * STEP, STEP), STEP)
        frames = fr[at, :].astype(F32)
        for degree in range(5):
            reach = min(degree, 2)
            breadth = 2 * degree + 1
            inputs = [gp[at, lanes(degree * degree + f)] for f in range(breadth)]
            for order in range(-reach, reach + 1):
                total = None
                for f in range(breadth):
                    i = INDEX[(degree, order, f)]
                    col = ENTRIES[i][3]
                    value = jnp.broadcast_to(frames[:, col : col + 1], (STEP, LANES))
                    fb[i, at, :] = value
                    term = value * inputs[f]
                    total = term if total is None else total + term
                mg[at, lanes(column(degree, order))] = total
        return 0

    lax.fori_loop(0, edges // STEP, message_step, 0)

    shared = [
        remote(halo.at[s, i], halo.at[s, i], halo_send.at[2 + i], halo_recv.at[2 + i], {"sub": other})
        for i in range(2)
    ]
    for i in range(2):
        halos[i].wait()
        shared[i].start()
    for copy in shared:
        copy.wait()
    for k in range(25):
        h = 0 if k < 13 else 1
        at = lanes(k - 12 * h)
        block = jnp.concatenate([halo[h, 0, :, at], nf[:, lanes(k)], halo[h, 1, :, at]], axis=0)
        sr[:, lanes(k)] = fast(pick_src, block)

    def rotate_step(c, _):
        at = pl.ds(pl.multiple_of(c * STEP, STEP), STEP)
        for degree in range(5):
            reach = min(degree, 2)
            breadth = 2 * degree + 1
            inputs = [sr[at, lanes(degree * degree + f)] for f in range(breadth)]
            for order in range(-reach, reach + 1):
                total = None
                for f in range(breadth):
                    term = fb[INDEX[(degree, order, f)], at, :] * inputs[f]
                    total = term if total is None else total + term
                zz[at, lanes(column(degree, order))] = total.astype(BF16)
        return 0

    lax.fori_loop(0, edges // STEP, rotate_step, 0)

    for load in loads:
        load.wait()
    z0 = zz[:, lanes(0, 5)]
    zp1, zm1 = zz[:, lanes(5, 4)], zz[:, lanes(9, 4)]
    zp2, zm2 = zz[:, lanes(13, 3)], zz[:, lanes(16, 3)]
    y0 = fast(z0, w0[...])
    scalar = y0[:, :LANES]
    vv[:, lanes(0, 5)] = y0.astype(BF16)
    vv[:, lanes(5, 4)] = (fast(zp1, w1[0]) - fast(zm1, w1[1])).astype(BF16)
    vv[:, lanes(9, 4)] = (fast(zp1, w1[1]) + fast(zm1, w1[0])).astype(BF16)
    vv[:, lanes(13, 3)] = (fast(zp2, w2[0]) - fast(zm2, w2[1])).astype(BF16)
    vv[:, lanes(16, 3)] = (fast(zp2, w2[1]) + fast(zm2, w2[0])).astype(BF16)
    bias_lanes = lax.dot_general(
        bias[...], tile_heads, (((0,), (0,)), ((), ())),
        preferred_element_type=F32, precision=lax.Precision.HIGHEST,
    )
    sigmoid = lax.logistic(scalar)
    gate = (scalar * sigmoid).astype(BF16)
    logits = fast(gate, alpha_t) + bias_lanes
    logits = jnp.where(mine, logits, -1e30)
    product = None
    for k in range(19):
        term = mg[:, lanes(k)] * vv[:, lanes(k)].astype(F32)
        product = term if product is None else product + term
    head_grad = exact(product, gather_heads)
    peak = jnp.max(logits, axis=0, keepdims=True)
    raised = jnp.where(mine, jnp.exp(logits - peak), 0.0)
    total = jnp.sum(raised, axis=0, keepdims=True)
    dots = jnp.sum(raised * head_grad, axis=0, keepdims=True)
    small[0:1, :] = peak
    small[1:2, :] = total
    small[2:3, :] = dots
    small[3:8, :] = jnp.zeros((5, LANES), F32)
    small_copy = remote(small, small_in, small_send, small_recv, {"sub": other})
    small_copy.start()

    weight[...] = exact(raised, spread)

    def back_step(c, _):
        at = pl.ds(pl.multiple_of(c * STEP, STEP), STEP)
        scale = weight[at, :]
        for degree in range(5):
            reach = min(degree, 2)
            orders = range(-reach, reach + 1)
            inputs = {o: vv[at, lanes(column(degree, o))].astype(F32) * scale for o in orders}
            for f in range(2 * degree + 1):
                out = None
                for o in orders:
                    term = fb[INDEX[(degree, o, f)], at, :] * inputs[o]
                    out = term if out is None else out + term
                bk[at, lanes(degree * degree + f)] = out.astype(BF16)
        return 0

    lax.fori_loop(0, edges // STEP, back_step, 0)
    small_copy.wait()
    peak_in = small_in[0:1, :]
    top = jnp.maximum(peak, peak_in)
    own_scale = jnp.exp(peak - top)
    in_scale = jnp.exp(peak_in - top)
    whole = total * own_scale + small_in[1:2, :] * in_scale
    all_dots = (dots * own_scale + small_in[2:3, :] * in_scale) / whole
    node_lane = lax.broadcasted_iota(jnp.int32, (rows_dev, LANES), 1)
    node_row = lax.broadcasted_iota(jnp.int32, (rows_dev, LANES), 0)
    node_scale = exact(
        jnp.where(lax.shift_right_logical(node_lane, 3) == node_row, own_scale / whole, 0.0), spread
    )
    for k in range(25):
        acc_out[:, lanes(k)] = fast(put_dst, bk[:, lanes(k)]) * node_scale
    acc_copy = remote(acc_out, acc_in, acc_send, acc_recv, {"sub": other})
    acc_copy.start()

    attention = raised * (own_scale / whole)
    logit_grad = (attention * (head_grad - all_dots)).astype(BF16)
    spread_att = exact(attention, spread)
    gate_grad = across(logit_grad, alpha_t) * sigmoid * (1.0 + scalar * (1.0 - sigmoid))
    for k in range(19):
        grad = mg[:, lanes(k)] * spread_att
        if k == 0:
            grad = grad + gate_grad
        gg[:, lanes(k)] = grad.astype(BF16)

    groups = graphs * 2

    def put(piece, base, rows_share, row0, matrix):
        wide = matrix.shape[1] // LANES
        part = wg[piece].shape[3]
        for i in range(matrix.shape[0] // STEP):
            row = row0 + i * STEP
            group = row // rows_share
            inner_row = (row % rows_share) // STEP
            for j in range(wide):
                tile = base + inner_row * wide + j
                wg[piece][group % 2, tile // part, group // 2, tile % part] = matrix[
                    i * STEP : (i + 1) * STEP, lanes(j)
                ].astype(BF16)

    def zero_tail(piece, used):
        part = wg[piece].shape[3]
        for tile in range(used, part * dps):
            wg[piece][:, tile // part, :, tile % part] = jnp.zeros((2, graphs, STEP, LANES), BF16)

    def stage_one(piece):
        return remote(
            wg[piece].at[other], r1[piece], s1s.at[piece], s1r.at[piece], {"sub": other}
        )

    def stage_two(piece):
        return [
            remote(
                hh[piece].at[dp_along(k)], r2[piece].at[k - 1],
                s2s.at[piece, k - 1], s2r.at[piece, k - 1], {"dp": dp_along(k)},
            )
            for k in range(1, dps)
        ]

    def stage_three(piece):
        return [
            remote(
                kk[piece].at[along(k)], r3[piece].at[k - 1],
                s3s.at[piece, k - 1], s3r.at[piece, k - 1], {"graph": along(k)},
            )
            for k in range(1, graphs)
        ]

    def stage_four(piece):
        return [
            remote(
                fin[piece].at[0], fin[piece].at[k],
                s4s.at[piece, k - 1], s4r.at[piece, k - 1], {"dp": dp_along(k)},
            )
            for k in range(1, dps)
        ]

    def start(copies):
        for copy in copies:
            copy.start()
        return copies

    def wait(copies):
        for copy in copies:
            copy.wait()

    gp1, gm1 = gg[:, lanes(5, 4)], gg[:, lanes(9, 4)]
    rows1 = 512 // groups
    one = [None] * 5
    tiles1 = (rows1 // STEP) * 4
    for b in range(4):
        put(0, 0, rows1, b * LANES, inner(zz[:, lanes(5 + b)], gp1) + inner(zz[:, lanes(9 + b)], gm1))
    zero_tail(0, tiles1)
    one[0] = stage_one(0)
    one[0].start()
    for b in range(4):
        put(1, 0, rows1, b * LANES, inner(zz[:, lanes(5 + b)], gm1) - inner(zz[:, lanes(9 + b)], gp1))
    zero_tail(1, tiles1)
    one[1] = stage_one(1)
    one[1].start()

    g0 = gg[:, lanes(0, 5)]
    rows0 = 640 // groups
    for b in range(5):
        put(2, 0, rows0, b * LANES, inner(zz[:, lanes(b)], g0))
    alpha_rows = LANES // groups
    tiles0 = (rows0 // STEP) * 5
    logit_small = fast(logit_grad, compact).astype(BF16)
    put(2, tiles0, alpha_rows, 0, inner(gate, logit_small))
    zero_tail(2, tiles0 + alpha_rows // STEP)
    one[2] = stage_one(2)
    one[2].start()

    def add_one(piece):
        one[piece].wait()
        for p in range(dps):
            hh[piece][p] = wg[piece][s, p] + r1[piece][p]
        return start(stage_two(piece))

    def add_two(piece):
        wait(two[piece])
        if dps == 2:
            kk[piece][...] = hh[piece][d] + r2[piece][0]
        else:
            value = hh[piece][d].astype(F32)
            for k in range(1, dps):
                value = value + r2[piece][k - 1].astype(F32)
            kk[piece][...] = value.astype(BF16)
        return start(stage_three(piece))

    def add_three(piece):
        wait(three[piece])
        value = kk[piece][g].astype(F32)
        for k in range(1, graphs):
            value = value + r3[piece][k - 1].astype(F32)
        fin[piece][0] = value.astype(BF16)
        return start(stage_four(piece))

    two = [None] * 5
    three = [None] * 5
    four = [None] * 5
    two[0] = add_one(0)

    acc_copy.wait()
    summed = jnp.concatenate(
        [(acc_out[:, lanes(k)] + acc_in[:, lanes(k)]).astype(BF16) for k in range(25)], axis=0
    )
    cotangent = jnp.concatenate([go[:, lanes(k)] for k in range(25)], axis=0)
    half = rows_dev // 2
    in_half = lax.broadcasted_iota(jnp.int32, summed.shape, 0)
    in_half = lax.shift_right_logical(jnp.bitwise_and(in_half, rows_dev - 1), 3) == s
    share = jnp.where(in_half, summed.astype(F32), 0.0).astype(BF16)
    gp2, gm2 = gg[:, lanes(13, 3)], gg[:, lanes(16, 3)]
    rows2 = 384 // groups
    tiles2 = (rows2 // STEP) * 3
    for b in range(3):
        put(3, 0, rows2, b * LANES, inner(zz[:, lanes(13 + b)], gp2) + inner(zz[:, lanes(16 + b)], gm2))
    zero_tail(3, tiles2)
    one[3] = stage_one(3)
    one[3].start()
    two[1] = add_one(1)
    for b in range(3):
        put(4, 0, rows2, b * LANES, inner(zz[:, lanes(13 + b)], gm2) - inner(zz[:, lanes(16 + b)], gp2))
    put(4, tiles2, alpha_rows, 0, inner(share, cotangent))
    zero_tail(4, tiles2 + alpha_rows // STEP)
    one[4] = stage_one(4)
    one[4].start()

    ig[:, lanes(0, 5)] = across(g0, w0[...]).astype(BF16)
    ig[:, lanes(5, 4)] = (across(gp1, w1[0]) + across(gm1, w1[1])).astype(BF16)
    two[2] = add_one(2)
    ig[:, lanes(9, 4)] = (across(gm1, w1[0]) - across(gp1, w1[1])).astype(BF16)
    ig[:, lanes(13, 3)] = (across(gp2, w2[0]) + across(gm2, w2[1])).astype(BF16)
    ig[:, lanes(16, 3)] = (across(gm2, w2[0]) - across(gp2, w2[1])).astype(BF16)
    two[3] = add_one(3)
    two[4] = add_one(4)

    def row_step(c, _):
        at = pl.ds(pl.multiple_of(c * STEP, STEP), STEP)
        for degree in range(5):
            reach = min(degree, 2)
            orders = range(-reach, reach + 1)
            inputs = {o: ig[at, lanes(column(degree, o))].astype(F32) for o in orders}
            for f in range(2 * degree + 1):
                out = None
                for o in orders:
                    term = fb[INDEX[(degree, o, f)], at, :] * inputs[o]
                    out = term if out is None else out + term
                rg[at, lanes(degree * degree + f)] = out.astype(BF16)
        return 0

    lax.fori_loop(0, edges // STEP, row_step, 0)

    three[0] = add_two(0)
    for k in range(13):
        low = fast(put_src, rg[:, lanes(k)])
        high = fast(put_src, rg[:, lanes(13 + k)]) if k < 12 else jnp.zeros_like(low)
        for b in range(3):
            for h in range(2):
                at = slice(b * rows_dev + h * half, b * rows_dev + (h + 1) * half)
                ng[h, b, :, lanes(k)] = jnp.concatenate([low[at], high[at]], axis=0).astype(BF16)
    node_core = remote(ng.at[other], ng_core, ng_send.at[0], ng_recv.at[0], {"sub": other})
    node_core.start()
    three[1] = add_two(1)
    node_core.wait()
    ng_sum[...] = ng[s] + ng_core[...]
    node_copies = [
        remote(ng_sum.at[2 * i], ng_in.at[i], ng_send.at[1 + i], ng_recv.at[1 + i], {"graph": along(step)})
        for i, step in enumerate((-1, 1))
    ]
    start(node_copies)

    projected = fast(summed, proj)
    for k in range(25):
        upd[:, lanes(k)] = (
            nf[:, lanes(k)].astype(F32) + projected[k * rows_dev : (k + 1) * rows_dev]
        ).astype(BF16)
    three[2] = add_two(2)

    three[3] = add_two(3)
    four[0] = add_three(0)
    three[4] = add_two(4)
    wait(node_copies)
    for k in range(13):
        value = ng[s, 1, :, lanes(k)].astype(F32) + ng_core[1, :, lanes(k)].astype(F32)
        value = value + ng_in[0, :, lanes(k)].astype(F32) + ng_in[1, :, lanes(k)].astype(F32)
        for part, coef in ((0, k), (1, 13 + k)):
            if coef < 25:
                base = go[:, lanes(coef)].astype(F32)
                base = jnp.where(s == 0, base[:half], base[half:])
                gn[:, lanes(coef)] = value[part * half : (part + 1) * half] + base

    for piece in range(1, 5):
        four[piece] = add_three(piece)
    base = 0
    for piece, count in enumerate(
        (tiles1, tiles1, tiles0 + alpha_rows // STEP, tiles2, tiles2 + alpha_rows // STEP)
    ):
        wait(four[piece])
        part = fin[piece].shape[1]
        for p in range(dps):
            size = min(part, count - p * part)
            if size > 0:
                at = base + p * part
                tiles_out[at : at + size] = fin[piece][lax.rem(d - p + dps, dps), :size]
        base += count


def unpack(upd, gn, tiles, upd_out, gn_out, o0, o1, o2, oa, oproj):
    upd_out[...] = upd[...]
    gn_out[...] = gn[...]
    base = 0

    def matrix(write, rows, wide):
        nonlocal base
        for i in range(rows // STEP):
            for j in range(wide):
                write(slice(i * STEP, (i + 1) * STEP), lanes(j), tiles[base].astype(F32))
                base += 1

    def into(ref, lead=None):
        def write(rows, columns, value):
            if lead is None:
                ref[rows, columns] = value
            else:
                ref[lead, rows, columns] = value

        return write

    for q in range(2):
        matrix(into(o1, q), o1.shape[1], 4)
    matrix(into(o0), o0.shape[0], 5)
    for i in range(oa.shape[1] // STEP):
        pick = lax.broadcasted_iota(jnp.int32, (oa.shape[0], LANES), 0) == lax.broadcasted_iota(
            jnp.int32, (oa.shape[0], LANES), 1
        )
        oa[:, i * STEP : (i + 1) * STEP] = across(
            jnp.where(pick, 1.0, 0.0).astype(BF16), tiles[base]
        )
        base += 1
    for q in range(2):
        matrix(into(o2, q), o2.shape[1], 3)
    matrix(into(oproj), oproj.shape[0], 1)


def fused_body(graphs, dps, parts):
    groups = graphs * 2

    def run(node_feats, frame_blocks, src_ids, dst_ids, edge_bias, w_zero, w_one, w_two, alpha_w, out_proj, grad_out):
        rows_dev = node_feats.shape[1]
        edges = frame_blocks.shape[1]
        heads = alpha_w.shape[1]
        used = (
            (512 // groups // STEP) * 4,
            (512 // groups // STEP) * 4,
            (640 // groups // STEP) * 5 + LANES // groups // STEP,
            (384 // groups // STEP) * 3,
            (384 // groups // STEP) * 3 + LANES // groups // STEP,
        )
        part = [-(-count // dps) for count in used]
        dma = pltpu.SemaphoreType.DMA
        wide = 25 * LANES
        kept = 19 * LANES

        def per_piece(lead):
            return [pltpu.VMEM((*lead(p), STEP, LANES), BF16) for p in part]

        scratch = [
            pltpu.VMEM(w_zero.shape, BF16),
            pltpu.VMEM(w_one.shape, BF16),
            pltpu.VMEM(w_two.shape, BF16),
            pltpu.VMEM((2, 2, rows_dev, 13 * LANES), BF16),
            pltpu.VMEM((8, LANES), F32),
            pltpu.VMEM((8, LANES), F32),
            pltpu.VMEM((rows_dev, wide), F32),
            pltpu.VMEM((rows_dev, wide), F32),
            pltpu.VMEM((len(ENTRIES), edges, LANES), F32),
            pltpu.VMEM((edges, wide), F32),
            pltpu.VMEM((edges, wide), F32),
            pltpu.VMEM((edges, kept), F32),
            pltpu.VMEM((edges, kept), BF16),
            pltpu.VMEM((edges, kept), BF16),
            pltpu.VMEM((edges, LANES), F32),
            pltpu.VMEM((edges, wide), BF16),
            pltpu.VMEM((edges, kept), BF16),
            pltpu.VMEM((edges, kept), BF16),
            pltpu.VMEM((edges, wide), BF16),
            pltpu.VMEM((2, 3, STEP, 13 * LANES), BF16),
            pltpu.VMEM((3, STEP, 13 * LANES), BF16),
            pltpu.VMEM((3, STEP, 13 * LANES), BF16),
            pltpu.VMEM((2, STEP, 13 * LANES), BF16),
            per_piece(lambda p: (2, dps, graphs, p)),
            per_piece(lambda p: (dps, graphs, p)),
            per_piece(lambda p: (dps, graphs, p)),
            per_piece(lambda p: (max(dps - 1, 1), graphs, p)),
            per_piece(lambda p: (graphs, p)),
            per_piece(lambda p: (graphs - 1, p)),
            per_piece(lambda p: (dps, p)),
            dma((3,)), dma((4,)), dma((4,)), dma, dma, dma, dma, dma((3,)), dma((3,)),
            dma((5,)), dma((5,)),
            dma((5, max(dps - 1, 1))), dma((5, max(dps - 1, 1))),
            dma((5, graphs - 1)), dma((5, graphs - 1)),
            dma((5, max(dps - 1, 1))), dma((5, max(dps - 1, 1))),
        ]
        flat = []
        counts = []
        for item in scratch:
            if isinstance(item, list):
                counts.append(len(item))
                flat.extend(item)
            else:
                counts.append(0)
                flat.append(item)

        def entry(*refs):
            lead, rest = refs[:14], list(refs[14:])
            grouped = []
            for count in counts:
                if count:
                    grouped.append(rest[:count])
                    rest = rest[count:]
                else:
                    grouped.append(rest.pop(0))
            fused(graphs, dps, parts, *lead, *grouped)

        vmem = pl.BlockSpec(memory_space=pltpu.VMEM)
        anywhere = pl.BlockSpec(memory_space=pl.ANY)
        count = sum(used)
        packed = pl.pallas_call(
            entry,
            out_shape=(
                jax.ShapeDtypeStruct((rows_dev, wide), BF16),
                jax.ShapeDtypeStruct((rows_dev // 2, wide), F32),
                jax.ShapeDtypeStruct((count, STEP, LANES), BF16),
            ),
            in_specs=[vmem] * 5 + [anywhere] * 3 + [vmem] * 3,
            out_specs=[vmem] * 3,
            scratch_shapes=flat,
            compiler_params=pltpu.CompilerParams(
                collective_id=0, has_side_effects=True, vmem_limit_bytes=56 * 1024 * 1024
            ),
        )(
            node_feats[0], frame_blocks[0], src_ids, dst_ids, edge_bias[0].T,
            w_zero, w_one, w_two, alpha_w.T, out_proj, grad_out[0],
        )
        out = pl.pallas_call(
            unpack,
            out_shape=(
                jax.ShapeDtypeStruct((rows_dev, wide), BF16),
                jax.ShapeDtypeStruct((rows_dev // 2, wide), F32),
                jax.ShapeDtypeStruct((640 // groups, 640), F32),
                jax.ShapeDtypeStruct((2, 512 // groups, 512), F32),
                jax.ShapeDtypeStruct((2, 384 // groups, 384), F32),
                jax.ShapeDtypeStruct((heads, LANES // groups), F32),
                jax.ShapeDtypeStruct((LANES // groups, LANES), F32),
            ),
            in_specs=[vmem] * 3,
            out_specs=[vmem] * 7,
        )(*packed)
        return (out[0][None], out[1][None], out[2], out[3], out[4], out[5].T, out[6])

    return run


def solution(mesh):
    placed = (
        P(("parts", "dp"), "graph", None),
        P(("parts", "dp"), ("graph", "sub"), None),
        P(("parts", "dp"), ("graph", "sub")),
        P(("parts", "dp"), ("graph", "sub")),
        P(("parts", "dp"), ("graph", "sub"), None),
        P(),
        P(),
        P(),
        P(),
        P(),
        P(("parts", "dp"), "graph", None),
    )
    graphs, dps = mesh.shape["graph"], mesh.shape["dp"]
    aligned = (128 // (graphs * 2)) % STEP == 0 and graphs >= 4 and mesh.shape["sub"] == 2
    return jax.shard_map(
        fused_body(graphs, dps, mesh.shape["parts"]) if aligned else body,
        mesh=mesh,
        in_specs=placed,
        out_specs=(
            P(("parts", "dp"), "graph", None),
            P(("parts", "dp"), ("graph", "sub"), None),
            P(("parts", "graph", "sub"), None),
            P("parts", ("graph", "sub"), None),
            P("parts", ("graph", "sub"), None),
            P(("parts", "graph", "sub"), None),
            P(("parts", "graph", "sub"), None),
        ),
        check_vma=False,
    )
```
